32 devices in a mesh: gx: 4 (over z), gy: 4 (over y, x), gz: 2 (over core).
Axes of the slice: x: 2, y: 2, z: 4, core: 2. Of those that a mesh axis runs over, the one named last changes fastest.
Arguments:
- displacement: float32 [3, 32, 32, 256], P(None, 'gx', 'gy', 'gz'), may hold values from -0.15 to 0.15
- velocity: float32 [3, 32, 32, 256], P(None, 'gx', 'gy', 'gz'), may hold values from -0.2 to 0.2
- micromodulus: float32 [32, 32, 256], P('gx', 'gy', 'gz'), may hold values from 0.25 to 4
- damage_bits: int32 [12, 32, 32, 256], P(None, 'gx', 'gy', 'gz'), may hold values from 0 to 4095, as said below
Outputs:
- force_density: float32 [3, 32, 32, 256], P(None, 'gx', 'gy', 'gz')
- displacement_next: float32 [3, 32, 32, 256], P(None, 'gx', 'gy', 'gz')
- velocity_next: float32 [3, 32, 32, 256], P(None, 'gx', 'gy', 'gz')
The draws below stay inside these ranges and needn't reach their ends.
Inputs may be any that keep to these rules, and one draw needn't show every extreme that they name: `damage_bits`: bit b of word w (w = 0 to 5) flags forward bond 12 w + b of the node as broken, in the order of the steps; words 6 to 11 hold the flags of the opposite offsets in the same places. Only bits 0 to 11 are used, and only bit 0 in words 5 and 11. The flag of offset -d at node j equals the flag of offset d at node j - d, and is clear where j - d lies outside the grid.
All inputs are finite; a program needn't handle non-finite values.
Results may differ from the reference program's by a relative error of at most 0.00002.
Values sent between devices are 32-bit elements; how exact they have to be, the bound alone decides.
No kernel may reach another device: no remote copies, remote signals or barrier semaphores. Data moves between devices by JAX's collectives and lax.ppermute only.
A program may use at most 64 MiB of HBM per device.

```python
import math
import jax
import jax.numpy as jnp
from jax import lax

HORIZON = 3
NX = 32
NY = 32
NZ = 256


def forward_offsets(margin):
    forward = []
    for step_x in range(-margin, margin + 1):
        for step_y in range(-margin, margin + 1):
            for step_z in range(-margin, margin + 1):
                radius = step_x * step_x + step_y * step_y + step_z * step_z
                leading = step_x > 0 or (step_x == 0 and (step_y > 0 or (step_y == 0 and step_z > 0)))
                if 0 < radius <= margin * margin and leading:
                    forward.append((step_x, step_y, step_z))
    return forward


def draw_damage_bits(key, part):
    key = jax.random.fold_in(key, 7)
    margin = HORIZON
    word_list = [jnp.zeros((NX, NY, NZ), jnp.int32) for word_id in range(12)]
    corner = jnp.zeros((NX, NY, NZ), jnp.int32).at[0, 0, 0].set(1)
    for number, offset in enumerate(forward_offsets(margin)):
        drawn = (jax.random.randint(jax.random.fold_in(key, number), (NX, NY, NZ), 0, 5) == 0).astype(jnp.int32)
        broken = jnp.maximum(drawn, corner)
        padded = jnp.pad(broken, margin)
        mirrored = padded[margin - offset[0]:margin - offset[0] + NX, margin - offset[1]:margin - offset[1] + NY, margin - offset[2]:margin - offset[2] + NZ]
        word_list[number // 12] = word_list[number // 12] + jnp.left_shift(broken, number % 12)
        word_list[6 + number // 12] = word_list[6 + number // 12] + jnp.left_shift(mirrored, number % 12)
    return jnp.stack(word_list)


def shard_levels(stream_key, dims, cuts, smallest, largest):
    loudness, own = 1.0, jax.random.fold_in(stream_key, 6)
    for position, blocks in cuts:
        steps = jnp.exp(jax.random.uniform(jax.random.fold_in(own, position), (blocks,), jnp.float32, smallest / len(cuts), largest / len(cuts)))
        loudness = loudness * jnp.repeat(steps, dims[position] // blocks).reshape([-1 if axis == position else 1 for axis in range(len(dims))])
    return loudness


def setup_inputs(seed: int = 0) -> dict:
    arg_keys = jax.random.split(jax.random.key(seed), 5)
    return {
        "displacement": jnp.clip(jax.random.uniform(arg_keys[0], (3, NX, NY, NZ), jnp.float32, -0.15, 0.15) * shard_levels(arg_keys[0], (3, NX, NY, NZ), ((1, 4), (2, 4), (3, 2)), -0.4, 0.0), -0.15, 0.15),
        "velocity": jnp.clip(jax.random.uniform(arg_keys[1], (3, NX, NY, NZ), jnp.float32, -0.2, 0.2) * shard_levels(arg_keys[1], (3, NX, NY, NZ), ((1, 4), (2, 4), (3, 2)), -0.4, 0.0), -0.2, 0.2),
        "micromodulus": jnp.clip(jnp.exp(math.log(4.0) - 2.7725887 * jax.random.uniform(arg_keys[2], (NX, NY, NZ), jnp.float32) ** shard_levels(arg_keys[2], (NX, NY, NZ), ((0, 4), (1, 4), (2, 2)), -0.2, 0.2)), 0.25, 4.0),
        "damage_bits": draw_damage_bits(jax.random.fold_in(arg_keys[4], 71), 0),
    }


DT_STEP = 0.25
BOND_SCALE = 5.0

def bond_offsets(margin):
    forward = []
    for step_x in range(-margin, margin + 1):
        for step_y in range(-margin, margin + 1):
            for step_z in range(-margin, margin + 1):
                radius = step_x * step_x + step_y * step_y + step_z * step_z
                leading = step_x > 0 or (step_x == 0 and (step_y > 0 or (step_y == 0 and step_z > 0)))
                if 0 < radius <= margin * margin and leading:
                    forward.append((step_x, step_y, step_z))
    return forward

def bond_force(own_disp, far_disp, root_own, root_far, intact, offset, length):
    stretch_x = offset[0] + far_disp[0] - own_disp[0]
    stretch_y = offset[1] + far_disp[1] - own_disp[1]
    stretch_z = offset[2] + far_disp[2] - own_disp[2]
    current = jnp.sqrt(stretch_x * stretch_x + stretch_y * stretch_y + stretch_z * stretch_z)
    factor = BOND_SCALE * root_own * root_far * intact * (current - length) / (length * length * current)
    return jnp.stack([factor * stretch_x, factor * stretch_y, factor * stretch_z])

def reference(displacement, velocity, micromodulus, damage_bits):
    margin = HORIZON
    advanced = displacement + DT_STEP * velocity
    root_mod = jnp.sqrt(micromodulus)
    widths = ((0, 0), (margin, margin), (margin, margin), (margin, margin))
    padded = jnp.pad(jnp.concatenate([advanced, root_mod[None]], axis=0), widths)
    forward = bond_offsets(margin)
    forward_count = len(forward)
    backward = [(-entry[0], -entry[1], -entry[2]) for entry in forward]
    offsets = forward + backward
    word_ids = [number // 12 for number in range(forward_count)] + [6 + number // 12 for number in range(forward_count)]
    bit_ids = [number % 12 for number in range(forward_count)] * 2
    squares = [entry[0] * entry[0] + entry[1] * entry[1] + entry[2] * entry[2] for entry in offsets]
    offset_table = jnp.asarray(offsets, jnp.int32)
    word_table = jnp.asarray(word_ids, jnp.int32)
    bit_table = jnp.asarray(bit_ids, jnp.int32)
    length_table = jnp.sqrt(jnp.asarray(squares, jnp.int32).astype(jnp.float32))
    extent = (4,) + advanced.shape[1:]

    def accumulate(bond_id, summed):
        offset = offset_table[bond_id]
        starts = (jnp.int32(0),) + tuple(((margin + offset[axis_id]).astype(jnp.int32) for axis_id in range(3)))
        window = lax.dynamic_slice(padded, starts, extent)
        flag_word = lax.dynamic_index_in_dim(damage_bits, word_table[bond_id], 0, keepdims=False)
        intact = 1.0 - jnp.bitwise_and(jnp.right_shift(flag_word, bit_table[bond_id]), 1).astype(jnp.float32)
        offset_real = offset.astype(jnp.float32)
        return summed + bond_force(advanced, window[:3], root_mod, window[3], intact, offset_real, length_table[bond_id])
    summed = lax.fori_loop(0, 2 * forward_count, accumulate, jnp.zeros_like(advanced))
    return (summed, advanced, velocity + DT_STEP * summed)
```

```python
import functools

import jax
import jax.numpy as jnp
from jax import lax
from jax.experimental import pallas as pl
from jax.experimental.pallas import tpu as pltpu
from jax.sharding import PartitionSpec as P

HORIZON = 3
DT_STEP = 0.25
BOND_SCALE = 5.0
LANES = 128
FRAME = 16
OWN = 4
RIM = 24


def bond_table():
    table = {}
    number = 0
    reach = range(-HORIZON, HORIZON + 1)
    for dx in reach:
        for dy in reach:
            for dz in reach:
                radius = dx * dx + dy * dy + dz * dz
                if 0 < radius <= HORIZON * HORIZON and (dx, dy, dz) > (0, 0, 0):
                    table[dx, dy, dz] = (number // 12, number % 12)
                    table[-dx, -dy, -dz] = (6 + number // 12, number % 12)
                    number += 1
    return table


BONDS = bond_table()


def lane_ids(rows):
    return lax.broadcasted_iota(jnp.int32, (rows, LANES), 1)


def rolled(block, shift):
    shift = shift % LANES
    return pltpu.roll(block, shift, axis=block.ndim - 1) if shift else block


def z_window(main, side, dz, wide):
    if not wide:
        return rolled(main, -dz)
    lane = lane_ids(main.shape[0])
    if dz > 0:
        return rolled(jnp.where(lane < dz, side, main), -dz)
    return rolled(jnp.where(lane >= LANES + dz, side, main), -dz)


def pack_margins(rows):
    lane = lane_ids(8)
    packed = jnp.zeros((8, LANES), jnp.float32)
    for group in range(3):
        moved = rolled(rows[8 * group : 8 * group + 8], 2 + 8 * group)
        packed = jnp.where((lane >= 8 * group) & (lane < 8 * group + 4), moved, packed)
    return packed


def unpack_margins(packed, group):
    lane = lane_ids(8)
    moved = rolled(packed, -(2 + 8 * group))
    return jnp.where((lane >= 126) | (lane < 2), moved, 0.0)


def advance_kernel(cells_z, disp, vel, mod, adv_out, root_out, msg_out):
    lane = lane_ids(8)
    for field in range(4):
        packed = jnp.zeros((8, LANES), jnp.float32)
        for x in range(8):
            if field < 3:
                own = disp[field, x] + DT_STEP * vel[field, x]
                adv_out[field, x] = own
            else:
                own = jnp.sqrt(mod[x])
                root_out[x] = own
            top = rolled(own, 8 * x - (cells_z - 3))
            low = rolled(own, 64 + 8 * x)
            packed = jnp.where((lane >= 8 * x) & (lane < 8 * x + 3), top, packed)
            packed = jnp.where((lane >= 64 + 8 * x) & (lane < 64 + 8 * x + 3), low, packed)
        msg_out[field] = packed


def side_kernel(cells_z, adv, root, arrived, main_out, side_out, low_out, top_out, hold):
    wide = cells_z == LANES
    lane = lane_ids(8)
    first = cells_z % LANES
    for field in range(4):
        got = arrived[field]
        for x in range(8):
            own = adv[field, x] if field < 3 else root[x]
            below = rolled(got, 125 - 8 * x)
            above = rolled(got, first - (64 + 8 * x))
            side = jnp.where((lane >= first) & (lane < first + 3), above, 0.0)
            side = jnp.where(lane >= 125, below, side)
            if not wide:
                own = jnp.where(lane < cells_z, own, side)
            main_out[field, x] = own
            side_out[field, x] = side
            low_out[field, 3 * x : 3 * x + 3] = own[:3]
            top_out[field, 3 * x : 3 * x + 3] = own[5:]
            if wide:
                hold[0, 3 * x : 3 * x + 3] = side[:3]
                hold[1, 3 * x : 3 * x + 3] = side[5:]
        if wide:
            low_out[field, RIM:] = pack_margins(hold[0])
            top_out[field, RIM:] = pack_margins(hold[1])


def frame_kernel(wide, main, side, below, above, main_out, side_out, low_out, top_out, hold):
    for field in range(4):
        if wide:
            for group in range(3):
                hold[0, 8 * group : 8 * group + 8] = unpack_margins(below[field, RIM:], group)
                hold[1, 8 * group : 8 * group + 8] = unpack_margins(above[field, RIM:], group)
        for x in range(8):
            main_out[field, x, :1] = jnp.zeros((1, LANES), jnp.float32)
            main_out[field, x, 1:OWN] = below[field, 3 * x : 3 * x + 3]
            main_out[field, x, OWN : OWN + 8] = main[field, x]
            main_out[field, x, OWN + 8 : 15] = above[field, 3 * x : 3 * x + 3]
            main_out[field, x, 15:] = jnp.zeros((1, LANES), jnp.float32)
            if wide:
                side_out[field, x, :1] = jnp.zeros((1, LANES), jnp.float32)
                side_out[field, x, 1:OWN] = hold[0, 3 * x : 3 * x + 3]
                side_out[field, x, OWN : OWN + 8] = side[field, x]
                side_out[field, x, OWN + 8 : 15] = hold[1, 3 * x : 3 * x + 3]
                side_out[field, x, 15:] = jnp.zeros((1, LANES), jnp.float32)
        for out, layers in ((low_out, (0, 1, 2)), (top_out, (7, 6, 5))):
            out[field, :12] = main_out[field, layers[0], 2:14]
            out[field, 12:24] = main_out[field, layers[1], 2:14]
            out[field, 24:32] = main_out[field, layers[2], OWN : OWN + 8]
            if wide:
                hold[2, :12] = side_out[field, layers[0], 2:14]
                hold[2, 12:24] = side_out[field, layers[1], 2:14]
                out[field, 32:] = pack_margins(hold[2])


def bond_sum(dx, own, words, far, total):
    from_x = own[0] - float(dx)
    from_z = {dz: own[2] - float(dz) for dz in range(-HORIZON, HORIZON + 1)}
    for dy in range(-HORIZON, HORIZON + 1):
        from_y = own[1] - float(dy)
        for dz in range(-HORIZON, HORIZON + 1):
            if (dx, dy, dz) not in BONDS:
                continue
            radius = float(dx * dx + dy * dy + dz * dz)
            word, bit = BONDS[dx, dy, dz]
            there = far(dy, dz)
            stretch_x = there[0] - from_x
            stretch_y = there[1] - from_y
            stretch_z = there[2] - from_z[dz]
            inverse = lax.rsqrt(stretch_x * stretch_x + stretch_y * stretch_y + stretch_z * stretch_z)
            factor = (BOND_SCALE / radius - (BOND_SCALE / radius**0.5) * inverse) * there[3]
            factor = jnp.where((words(word) & (1 << bit)) == 0, factor, 0.0)
            total = (
                total[0] + factor * stretch_x,
                total[1] + factor * stretch_y,
                total[2] + factor * stretch_z,
            )
    return total


SHIFTS = (-2, -1, 1, 2)


def inner_kernel(wide, main, side, bits, total_out, near, far):
    for field in range(4):
        for x in range(8):
            for half in range(2):
                rows = slice(8 * half, 8 * half + 8)
                block = main[field, x, rows]
                margin = side[field, x, rows] if wide else None
                for slot, dz in enumerate(SHIFTS):
                    near[slot, field, x, rows] = z_window(block, margin, dz, wide)
            rows = slice(OWN, OWN + 8)
            block = main[field, x, rows]
            margin = side[field, x, rows] if wide else None
            for slot, dz in enumerate((-3, 3)):
                far[slot, field, x] = z_window(block, margin, dz, wide)

    for dx in (0, -1, 1, -2, 2, -3, 3):

        def step(x, carry, dx=dx):
            own = [main[field, x, OWN : OWN + 8] for field in range(3)]

            def there(dy, dz):
                rows = slice(OWN + dy, OWN + dy + 8)
                if dz == 0:
                    return [main[field, x + dx, rows] for field in range(4)]
                if abs(dz) == 3:
                    return [far[int(dz > 0), field, x + dx] for field in range(4)]
                slot = SHIFTS.index(dz)
                return [near[slot, field, x + dx, rows] for field in range(4)]

            if dx == 0:
                total = (jnp.zeros((8, LANES), jnp.float32),) * 3
            else:
                total = tuple(total_out[field, x] for field in range(3))
            total = bond_sum(dx, own, lambda word: bits[word, x], there, total)
            for field in range(3):
                total_out[field, x] = total[field]
            return carry

        lax.fori_loop(max(0, -dx), min(8, 8 - dx), step, 0)


def outer_kernel(wide, main, below, above, bits, vel, partial, force_out, vel_out, layer, near, hold):
    for face, block in enumerate((below, above)):
        for field in range(4):
            layer[face, 0, field, 2:14] = block[field, :12]
            layer[face, 1, field, 2:14] = block[field, 12:24]
            if wide:
                for group in range(3):
                    hold[0, 8 * group : 8 * group + 8] = unpack_margins(block[field, 32:], group)
                hold[1, 2:14] = hold[0, :12]
                hold[2, 2:14] = hold[0, 12:24]
            for depth in range(2):
                for half in range(2):
                    rows = slice(8 * half, 8 * half + 8)
                    inner = layer[face, depth, field, rows]
                    margin = hold[1 + depth, rows] if wide else None
                    for slot, dz in enumerate(SHIFTS):
                        near[face, depth, slot, field, rows] = z_window(inner, margin, dz, wide)
    for x in range(8):
        total = tuple(partial[field, x] for field in range(3))
        own = [main[field, x, OWN : OWN + 8] for field in range(4)]
        for dx in range(-HORIZON, HORIZON + 1):
            if 0 <= x + dx < 8:
                continue
            face = 0 if dx < 0 else 1
            depth = -(x + dx) - 1 if dx < 0 else x + dx - 8
            block = below if dx < 0 else above

            def there(dy, dz, face=face, depth=depth, block=block):
                rows = slice(OWN + dy, OWN + dy + 8)
                if depth == 2:
                    return [block[field, 24:32] for field in range(4)]
                if dz == 0:
                    return [layer[face, depth, field, rows] for field in range(4)]
                slot = SHIFTS.index(dz)
                return [near[face, depth, slot, field, rows] for field in range(4)]

            total = bond_sum(dx, own, lambda word, x=x: bits[word, x], there, total)
        for field in range(3):
            force = own[3] * total[field]
            force_out[field, x] = force
            vel_out[field, x] = vel[field, x] + DT_STEP * force


def call(kernel, outs, scratch, flops, *operands):
    shapes = [jax.ShapeDtypeStruct(shape, jnp.float32) for shape in outs]
    moved = sum(4 * int(a.size) for a in operands) + sum(4 * int(a.size) for a in shapes)
    vmem = pl.BlockSpec(memory_space=pltpu.VMEM)
    return pl.pallas_call(
        kernel,
        out_shape=shapes,
        in_specs=[vmem] * len(operands),
        out_specs=[vmem] * len(shapes),
        scratch_shapes=[pltpu.VMEM(shape, jnp.float32) for shape in scratch],
        compiler_params=pltpu.CompilerParams(vmem_limit_bytes=24 * 1024 * 1024),
        cost_estimate=pl.CostEstimate(flops=flops, bytes_accessed=moved, transcendentals=0),
    )(*operands)


def traded(low, top, axis):
    count = lax.axis_size(axis)
    even = lax.axis_index(axis) % 2 == 0
    got = []
    for start, block in ((0, jnp.where(even, top, low)), (1, jnp.where(even, low, top))):
        pairs = []
        for i in range(start, count - 1, 2):
            pairs += [(i, i + 1), (i + 1, i)]
        got.append(lax.ppermute(block, axis, pairs) if pairs else jnp.zeros_like(block))
    return jnp.where(even, got[1], got[0]), jnp.where(even, got[0], got[1])


def body(displacement, velocity, micromodulus, damage_bits):
    cells_z = micromodulus.shape[2]
    wide = cells_z == LANES
    if not wide:
        pad = [(0, 0), (0, 0), (0, 0), (0, LANES - cells_z)]
        displacement, velocity, damage_bits = (
            jnp.pad(a, pad) for a in (displacement, velocity, damage_bits)
        )
        micromodulus = jnp.pad(micromodulus, pad[1:])
    brick = (8, 8, LANES)
    advanced, root, z_msg = call(
        functools.partial(advance_kernel, cells_z),
        [(3, *brick), brick, (4, 8, LANES)],
        [],
        100_000,
        displacement,
        velocity,
        micromodulus,
    )
    first_half = lax.broadcasted_iota(jnp.int32, z_msg.shape, 2) < 64
    count = lax.axis_size("gz")
    place = lax.axis_index("gz")
    if count == 2:
        other = lax.ppermute(z_msg, "gz", [(0, 1), (1, 0)])
        z_got = jnp.where(first_half == (place == 1), other, 0.0)
    else:
        before, after = traded(z_msg, z_msg, "gz")
        z_got = jnp.where(first_half, before, after)
    main, side, low, top = call(
        functools.partial(side_kernel, cells_z),
        [(4, *brick), (4, *brick), (4, RIM + 8, LANES), (4, RIM + 8, LANES)],
        [(2, RIM, LANES)],
        100_000,
        advanced,
        root,
        z_got,
    )
    below, above = traded(low, top, "gy")
    framed = (4, 8, FRAME, LANES)
    main, side, low, top = call(
        functools.partial(frame_kernel, wide),
        [framed, framed, (4, 40, LANES), (4, 40, LANES)],
        [(3, RIM, LANES)],
        100_000,
        main,
        side,
        below,
        above,
    )
    below, above = traded(low, top, "gx")
    (partial,) = call(
        functools.partial(inner_kernel, wide),
        [(3, *brick)],
        [(4, *framed), (2, 4, *brick)],
        20_000_000,
        main,
        side,
        damage_bits,
    )
    force, moved = call(
        functools.partial(outer_kernel, wide),
        [(3, *brick), (3, *brick)],
        [(2, 2, 4, FRAME, LANES), (2, 2, 4, 4, FRAME, LANES), (3, RIM, LANES)],
        4_000_000,
        main,
        below,
        above,
        damage_bits,
        velocity,
        partial,
    )
    return force[..., :cells_z], advanced[..., :cells_z], moved[..., :cells_z]


def solution(mesh):
    placed = P(None, "gx", "gy", "gz")
    return jax.shard_map(
        body,
        mesh=mesh,
        in_specs=(placed, placed, P("gx", "gy", "gz"), placed),
        out_specs=(placed, placed, placed),
        check_vma=False,
    )
```

```python
import functools

import jax
import jax.numpy as jnp
from jax import lax
from jax.experimental import pallas as pl
from jax.experimental.pallas import tpu as pltpu
from jax.sharding import PartitionSpec as P

HORIZON = 3
DT_STEP = 0.25
BOND_SCALE = 5.0
LANES = 128
FRAME = 16
OWN = 4
RIM = 24
DEEP = 32


def bond_table():
    table = {}
    number = 0
    reach = range(-HORIZON, HORIZON + 1)
    for dx in reach:
        for dy in reach:
            for dz in reach:
                radius = dx * dx + dy * dy + dz * dz
                if 0 < radius <= HORIZON * HORIZON and (dx, dy, dz) > (0, 0, 0):
                    table[dx, dy, dz] = (number // 12, number % 12)
                    table[-dx, -dy, -dz] = (6 + number // 12, number % 12)
                    number += 1
    return table


BONDS = bond_table()


def lane_ids(rows):
    return lax.broadcasted_iota(jnp.int32, (rows, LANES), 1)


def rolled(block, shift):
    shift = shift % LANES
    return pltpu.roll(block, shift, axis=block.ndim - 1) if shift else block


def z_window(main, side, dz, wide):
    if not wide:
        return rolled(main, -dz)
    lane = lane_ids(main.shape[0])
    if dz > 0:
        return rolled(jnp.where(lane < dz, side, main), -dz)
    return rolled(jnp.where(lane >= LANES + dz, side, main), -dz)


def pack_margins(packed, rows, field):
    lane = lane_ids(8)
    for group in range(3):
        start = 4 * (3 * field + group)
        moved = rolled(rows[8 * group : 8 * group + 8], 2 + start)
        packed = jnp.where((lane >= start) & (lane < start + 4), moved, packed)
    return packed


def unpack_margins(packed, field, group):
    lane = lane_ids(8)
    moved = rolled(packed, -(2 + 4 * (3 * field + group)))
    return jnp.where((lane >= 126) | (lane < 2), moved, 0.0)


def advance_kernel(cells_z, disp, vel, mod, field_out, vel_out, msg_out, hold, hold_mod, sem):
    copies = [
        pltpu.make_async_copy(disp, hold, sem.at[0]),
        pltpu.make_async_copy(vel, vel_out, sem.at[1]),
        pltpu.make_async_copy(mod, hold_mod, sem.at[2]),
    ]
    for copy in copies:
        copy.start()
    for copy in copies:
        copy.wait()
    lane = lane_ids(8)
    for field in range(4):
        packed = jnp.zeros((8, LANES), jnp.float32)
        for x in range(8):
            if field < 3:
                own = hold[field, x] + DT_STEP * vel_out[field, x]
            else:
                own = jnp.sqrt(hold_mod[x])
            field_out[field, x] = own
            top = rolled(own, 8 * x - (cells_z - 3))
            low = rolled(own, 64 + 8 * x)
            packed = jnp.where((lane >= 8 * x) & (lane < 8 * x + 3), top, packed)
            packed = jnp.where((lane >= 64 + 8 * x) & (lane < 64 + 8 * x + 3), low, packed)
        msg_out[field] = packed


def side_kernel(cells_z, fields, arrived, main_out, side_out, low_out, top_out, hold):
    wide = cells_z == LANES
    lane = lane_ids(8)
    first = cells_z % LANES
    packed = [jnp.zeros((8, LANES), jnp.float32)] * 2
    for field in range(4):
        got = arrived[field]
        for x in range(8):
            own = fields[field, x]
            below = rolled(got, 125 - 8 * x)
            above = rolled(got, first - (64 + 8 * x))
            side = jnp.where((lane >= first) & (lane < first + 3), above, 0.0)
            side = jnp.where(lane >= 125, below, side)
            if not wide:
                own = jnp.where(lane < cells_z, own, side)
            row = RIM * field + 3 * x
            main_out[field, x] = own
            side_out[field, x] = side
            low_out[row : row + 3] = own[:3]
            top_out[row : row + 3] = own[5:]
            if wide:
                hold[0, 3 * x : 3 * x + 3] = side[:3]
                hold[1, 3 * x : 3 * x + 3] = side[5:]
        if wide:
            packed = [pack_margins(packed[face], hold[face], field) for face in range(2)]
    low_out[4 * RIM :] = packed[0]
    top_out[4 * RIM :] = packed[1]


def frame_kernel(wide, main, side, below, above, main_out, side_out, low_out, top_out, hold):
    packed = [jnp.zeros((8, LANES), jnp.float32)] * 2
    for field in range(4):
        if wide:
            for face, block in enumerate((below, above)):
                for group in range(3):
                    rows = slice(8 * group, 8 * group + 8)
                    hold[face, rows] = unpack_margins(block[4 * RIM :], field, group)
        for x in range(8):
            row = RIM * field + 3 * x
            main_out[field, x, :1] = jnp.zeros((1, LANES), jnp.float32)
            main_out[field, x, 1:OWN] = below[row : row + 3]
            main_out[field, x, OWN : OWN + 8] = main[field, x]
            main_out[field, x, OWN + 8 : 15] = above[row : row + 3]
            main_out[field, x, 15:] = jnp.zeros((1, LANES), jnp.float32)
            if wide:
                side_out[field, x, :1] = jnp.zeros((1, LANES), jnp.float32)
                side_out[field, x, 1:OWN] = hold[0, 3 * x : 3 * x + 3]
                side_out[field, x, OWN : OWN + 8] = side[field, x]
                side_out[field, x, OWN + 8 : 15] = hold[1, 3 * x : 3 * x + 3]
                side_out[field, x, 15:] = jnp.zeros((1, LANES), jnp.float32)
        for face, (out, layers) in enumerate(((low_out, (0, 1, 2)), (top_out, (7, 6, 5)))):
            row = DEEP * field
            out[row : row + 12] = main_out[field, layers[0], 2:14]
            out[row + 12 : row + 24] = main_out[field, layers[1], 2:14]
            out[row + 24 : row + 32] = main_out[field, layers[2], OWN : OWN + 8]
            if wide:
                hold[2 + face, :12] = side_out[field, layers[0], 2:14]
                hold[2 + face, 12:24] = side_out[field, layers[1], 2:14]
                packed[face] = pack_margins(packed[face], hold[2 + face], field)
    low_out[4 * DEEP :] = packed[0]
    top_out[4 * DEEP :] = packed[1]


def bond_sum(dx, own, words, far, total):
    from_x = own[0] - float(dx)
    from_z = {dz: own[2] - float(dz) for dz in range(-HORIZON, HORIZON + 1)}
    for dy in range(-HORIZON, HORIZON + 1):
        from_y = own[1] - float(dy)
        for dz in range(-HORIZON, HORIZON + 1):
            if (dx, dy, dz) not in BONDS:
                continue
            radius = float(dx * dx + dy * dy + dz * dz)
            word, bit = BONDS[dx, dy, dz]
            there = far(dy, dz)
            stretch_x = there[0] - from_x
            stretch_y = there[1] - from_y
            stretch_z = there[2] - from_z[dz]
            inverse = lax.rsqrt(stretch_x * stretch_x + stretch_y * stretch_y + stretch_z * stretch_z)
            factor = (BOND_SCALE / radius - (BOND_SCALE / radius**0.5) * inverse) * there[3]
            factor = jnp.where((words(word) & (1 << bit)) == 0, factor, 0.0)
            total = (
                total[0] + factor * stretch_x,
                total[1] + factor * stretch_y,
                total[2] + factor * stretch_z,
            )
    return total


SHIFTS = (-2, -1, 1, 2)


def inner_kernel(wide, main, side, bits, fields, total_out, next_out, near, far, sem):
    copy = pltpu.make_async_copy(fields.at[:3], next_out, sem)
    copy.start()
    for field in range(4):
        for x in range(8):
            for half in range(2):
                rows = slice(8 * half, 8 * half + 8)
                block = main[field, x, rows]
                margin = side[field, x, rows] if wide else None
                for slot, dz in enumerate(SHIFTS):
                    near[slot, field, x, rows] = z_window(block, margin, dz, wide)
            rows = slice(OWN, OWN + 8)
            block = main[field, x, rows]
            margin = side[field, x, rows] if wide else None
            for slot, dz in enumerate((-3, 3)):
                far[slot, field, x] = z_window(block, margin, dz, wide)

    for dx in (0, -1, 1, -2, 2, -3, 3):

        def step(x, carry, dx=dx):
            own = [main[field, x, OWN : OWN + 8] for field in range(3)]

            def there(dy, dz):
                rows = slice(OWN + dy, OWN + dy + 8)
                if dz == 0:
                    return [main[field, x + dx, rows] for field in range(4)]
                if abs(dz) == 3:
                    return [far[int(dz > 0), field, x + dx] for field in range(4)]
                slot = SHIFTS.index(dz)
                return [near[slot, field, x + dx, rows] for field in range(4)]

            if dx == 0:
                total = (jnp.zeros((8, LANES), jnp.float32),) * 3
            else:
                total = tuple(total_out[field, x] for field in range(3))
            total = bond_sum(dx, own, lambda word: bits[word, x], there, total)
            for field in range(3):
                total_out[field, x] = total[field]
            return carry

        lax.fori_loop(max(0, -dx), min(8, 8 - dx), step, 0)
    copy.wait()


def outer_kernel(
    wide, main, below, above, bits, vel, partial, force_out, vel_out, layer, near, hold, force_buf, vel_buf, sem
):
    copies = []

    def finish(x, total, root):
        for field in range(3):
            force = root * total[field]
            force_buf[x, field] = force
            vel_buf[x, field] = vel[field, x] + DT_STEP * force
        for slot, (buf, out) in enumerate(((force_buf, force_out), (vel_buf, vel_out))):
            copies.append(pltpu.make_async_copy(buf.at[x], out.at[:, x], sem.at[slot, x]))
            copies[-1].start()

    for x in (3, 4):
        finish(x, [partial[field, x] for field in range(3)], main[3, x, OWN : OWN + 8])
    for face, block in enumerate((below, above)):
        for field in range(4):
            row = DEEP * field
            layer[face, 0, field, 2:14] = block[row : row + 12]
            layer[face, 1, field, 2:14] = block[row + 12 : row + 24]
            if wide:
                for group in range(3):
                    rows = slice(8 * group, 8 * group + 8)
                    hold[0, rows] = unpack_margins(block[4 * DEEP :], field, group)
                hold[1, 2:14] = hold[0, :12]
                hold[2, 2:14] = hold[0, 12:24]
            for depth in range(2):
                for half in range(2):
                    rows = slice(8 * half, 8 * half + 8)
                    inner = layer[face, depth, field, rows]
                    margin = hold[1 + depth, rows] if wide else None
                    for slot, dz in enumerate(SHIFTS):
                        near[face, depth, slot, field, rows] = z_window(inner, margin, dz, wide)
    for x in (2, 5, 1, 6, 0, 7):
        total = tuple(partial[field, x] for field in range(3))
        own = [main[field, x, OWN : OWN + 8] for field in range(4)]
        for dx in range(-HORIZON, HORIZON + 1):
            if 0 <= x + dx < 8:
                continue
            face = 0 if dx < 0 else 1
            depth = -(x + dx) - 1 if dx < 0 else x + dx - 8
            block = below if dx < 0 else above

            def there(dy, dz, face=face, depth=depth, block=block):
                rows = slice(OWN + dy, OWN + dy + 8)
                if depth == 2:
                    return [block[DEEP * field + 24 : DEEP * field + 32] for field in range(4)]
                if dz == 0:
                    return [layer[face, depth, field, rows] for field in range(4)]
                slot = SHIFTS.index(dz)
                return [near[face, depth, slot, field, rows] for field in range(4)]

            total = bond_sum(dx, own, lambda word, x=x: bits[word, x], there, total)
        finish(x, total, own[3])
    for copy in copies:
        copy.wait()


VMEM = pl.BlockSpec(memory_space=pltpu.VMEM)
HBM = pl.BlockSpec(memory_space=pltpu.HBM)


def call(kernel, ins, outs, scratch, flops, *operands):
    shapes = [jax.ShapeDtypeStruct(shape, jnp.float32) for shape, _ in outs]
    moved = sum(4 * int(a.size) for a in operands) + sum(4 * int(a.size) for a in shapes)
    return pl.pallas_call(
        kernel,
        out_shape=shapes,
        in_specs=ins,
        out_specs=[place for _, place in outs],
        scratch_shapes=[pltpu.VMEM(a, jnp.float32) if isinstance(a, tuple) else a for a in scratch],
        compiler_params=pltpu.CompilerParams(vmem_limit_bytes=24 * 1024 * 1024),
        cost_estimate=pl.CostEstimate(flops=flops, bytes_accessed=moved, transcendentals=0),
    )(*operands)


def traded(low, top, axis, middle_first):
    count = lax.axis_size(axis)
    even = lax.axis_index(axis) % 2 == 0
    got = []
    for start, block in ((0, jnp.where(even, top, low)), (1, jnp.where(even, low, top))):
        pairs = []
        for i in range(start, count - 1, 2):
            pairs += [(i, i + 1), (i + 1, i)]
        got.append(lax.ppermute(block, axis, pairs) if pairs else jnp.zeros_like(block))
    if middle_first:
        outer, middle = lax.optimization_barrier((got[0], got[1]))
    else:
        middle, outer = lax.optimization_barrier((got[1], got[0]))
    return jnp.where(even, middle, outer), jnp.where(even, outer, middle)


def body(displacement, velocity, micromodulus, damage_bits):
    cells_z = micromodulus.shape[2]
    wide = cells_z == LANES
    if not wide:
        pad = [(0, 0), (0, 0), (0, 0), (0, LANES - cells_z)]
        displacement, velocity, damage_bits = (
            jnp.pad(a, pad) for a in (displacement, velocity, damage_bits)
        )
        micromodulus = jnp.pad(micromodulus, pad[1:])
    brick = (8, 8, LANES)
    fields, kept, z_msg = call(
        functools.partial(advance_kernel, cells_z),
        [HBM] * 3,
        [((4, *brick), VMEM), ((3, *brick), VMEM), ((4, 8, LANES), VMEM)],
        [(3, *brick), brick, pltpu.SemaphoreType.DMA((3,))],
        100_000,
        *(pltpu.with_memory_space_constraint(a, pltpu.HBM) for a in (displacement, velocity, micromodulus)),
    )
    first_half = lax.broadcasted_iota(jnp.int32, z_msg.shape, 2) < 64
    count = lax.axis_size("gz")
    place = lax.axis_index("gz")
    if count == 2:
        other = lax.ppermute(z_msg, "gz", [(0, 1), (1, 0)])
        z_got = jnp.where(first_half == (place == 1), other, 0.0)
    else:
        before, after = traded(z_msg, z_msg, "gz", False)
        z_got = jnp.where(first_half, before, after)
    rim_msg = ((4 * RIM + 8, LANES), VMEM)
    main, side, low, top = call(
        functools.partial(side_kernel, cells_z),
        [VMEM] * 2,
        [((4, *brick), VMEM), ((4, *brick), VMEM), rim_msg, rim_msg],
        [(2, RIM, LANES)],
        100_000,
        fields,
        z_got,
    )
    below, above = traded(low, top, "gy", False)
    framed = (4, 8, FRAME, LANES)
    deep_msg = ((4 * DEEP + 8, LANES), VMEM)
    main, side, low, top = call(
        functools.partial(frame_kernel, wide),
        [VMEM] * 4,
        [(framed, VMEM), (framed, VMEM), deep_msg, deep_msg],
        [(4, RIM, LANES)],
        100_000,
        main,
        side,
        below,
        above,
    )
    below, above = traded(low, top, "gx", True)
    partial, advanced = call(
        functools.partial(inner_kernel, wide),
        [VMEM] * 4,
        [((3, *brick), VMEM), ((3, *brick), HBM)],
        [(4, *framed), (2, 4, *brick), pltpu.SemaphoreType.DMA],
        20_000_000,
        main,
        side,
        damage_bits,
        fields,
    )
    force, moved = call(
        functools.partial(outer_kernel, wide),
        [VMEM] * 6,
        [((3, *brick), HBM), ((3, *brick), HBM)],
        [
            (2, 2, 4, FRAME, LANES),
            (2, 2, 4, 4, FRAME, LANES),
            (3, RIM, LANES),
            (8, 3, 8, LANES),
            (8, 3, 8, LANES),
            pltpu.SemaphoreType.DMA((2, 8)),
        ],
        4_000_000,
        main,
        below,
        above,
        damage_bits,
        kept,
        partial,
    )
    return force[..., :cells_z], advanced[..., :cells_z], moved[..., :cells_z]


def solution(mesh):
    placed = P(None, "gx", "gy", "gz")
    return jax.shard_map(
        body,
        mesh=mesh,
        in_specs=(placed, placed, P("gx", "gy", "gz"), placed),
        out_specs=(placed, placed, placed),
        check_vma=False,
    )
```

```python
import functools

import jax
import jax.numpy as jnp
from jax import lax
from jax.experimental import pallas as pl
from jax.experimental.pallas import tpu as pltpu
from jax.sharding import PartitionSpec as P

HORIZON = 3
DT_STEP = 0.25
BOND_SCALE = 5.0
LANES = 128
FRAME = 16
OWN = 4
RIM = 24
DEEP = 32


def bond_table():
    table = {}
    number = 0
    reach = range(-HORIZON, HORIZON + 1)
    for dx in reach:
        for dy in reach:
            for dz in reach:
                radius = dx * dx + dy * dy + dz * dz
                if 0 < radius <= HORIZON * HORIZON and (dx, dy, dz) > (0, 0, 0):
                    table[dx, dy, dz] = (number // 12, number % 12)
                    table[-dx, -dy, -dz] = (6 + number // 12, number % 12)
                    number += 1
    return table


BONDS = bond_table()


def lane_ids(rows):
    return lax.broadcasted_iota(jnp.int32, (rows, LANES), 1)


def rolled(block, shift):
    shift = shift % LANES
    return pltpu.roll(block, shift, axis=block.ndim - 1) if shift else block


def z_window(main, side, dz, wide):
    if not wide:
        return rolled(main, -dz)
    lane = lane_ids(main.shape[0])
    if dz > 0:
        return rolled(jnp.where(lane < dz, side, main), -dz)
    return rolled(jnp.where(lane >= LANES + dz, side, main), -dz)


def pack_margins(packed, rows, field):
    lane = lane_ids(8)
    for group in range(3):
        start = 4 * (3 * field + group)
        moved = rolled(rows[8 * group : 8 * group + 8], 2 + start)
        packed = jnp.where((lane >= start) & (lane < start + 4), moved, packed)
    return packed


def unpack_margins(packed, field, group):
    lane = lane_ids(8)
    moved = rolled(packed, -(2 + 4 * (3 * field + group)))
    return jnp.where((lane >= 126) | (lane < 2), moved, 0.0)


def advance_kernel(cells_z, disp, vel, mod, field_out, vel_out, msg_out, hold, hold_mod, sem):
    copies = [
        pltpu.make_async_copy(disp, hold, sem.at[0]),
        pltpu.make_async_copy(vel, vel_out, sem.at[1]),
        pltpu.make_async_copy(mod, hold_mod, sem.at[2]),
    ]
    for copy in copies:
        copy.start()
    for copy in copies:
        copy.wait()
    lane = lane_ids(8)
    for field in range(4):
        packed = jnp.zeros((8, LANES), jnp.float32)
        for x in range(8):
            if field < 3:
                own = hold[field, x] + DT_STEP * vel_out[field, x]
            else:
                own = jnp.sqrt(hold_mod[x])
            field_out[field, x] = own
            top = rolled(own, 8 * x - (cells_z - 3))
            low = rolled(own, 64 + 8 * x)
            packed = jnp.where((lane >= 8 * x) & (lane < 8 * x + 3), top, packed)
            packed = jnp.where((lane >= 64 + 8 * x) & (lane < 64 + 8 * x + 3), low, packed)
        msg_out[field] = packed


def side_kernel(cells_z, fields, arrived, main_out, side_out, low_out, top_out, hold):
    wide = cells_z == LANES
    lane = lane_ids(8)
    first = cells_z % LANES
    packed = [jnp.zeros((8, LANES), jnp.float32)] * 2
    for field in range(4):
        got = arrived[field]
        for x in range(8):
            own = fields[field, x]
            below = rolled(got, 125 - 8 * x)
            above = rolled(got, first - (64 + 8 * x))
            side = jnp.where((lane >= first) & (lane < first + 3), above, 0.0)
            side = jnp.where(lane >= 125, below, side)
            if not wide:
                own = jnp.where(lane < cells_z, own, side)
            row = RIM * field + 3 * x
            main_out[field, x] = own
            side_out[field, x] = side
            low_out[row : row + 3] = own[:3]
            top_out[row : row + 3] = own[5:]
            if wide:
                hold[0, 3 * x : 3 * x + 3] = side[:3]
                hold[1, 3 * x : 3 * x + 3] = side[5:]
        if wide:
            packed = [pack_margins(packed[face], hold[face], field) for face in range(2)]
    low_out[4 * RIM :] = packed[0]
    top_out[4 * RIM :] = packed[1]


def deep_kernel(wide, main, side, below, above, low_out, top_out, hold):
    packed = [jnp.zeros((8, LANES), jnp.float32)] * 2
    for field in range(4):
        if wide:
            for face, block in enumerate((below, above)):
                for group in range(3):
                    rows = slice(8 * group, 8 * group + 8)
                    hold[face, rows] = unpack_margins(block[4 * RIM :], field, group)
        for face, (out, layers) in enumerate(((low_out, (0, 1, 2)), (top_out, (7, 6, 5)))):
            for depth, x in enumerate(layers[:2]):
                row = DEEP * field + 12 * depth
                rim = RIM * field + 3 * x
                out[row : row + 2] = below[rim + 1 : rim + 3]
                out[row + 2 : row + 10] = main[field, x]
                out[row + 10 : row + 12] = above[rim : rim + 2]
                if wide:
                    row = 12 * depth
                    hold[2 + face, row : row + 2] = hold[0, 3 * x + 1 : 3 * x + 3]
                    hold[2 + face, row + 2 : row + 10] = side[field, x]
                    hold[2 + face, row + 10 : row + 12] = hold[1, 3 * x : 3 * x + 2]
            out[DEEP * field + 24 : DEEP * field + 32] = main[field, layers[2]]
            if wide:
                packed[face] = pack_margins(packed[face], hold[2 + face], field)
    low_out[4 * DEEP :] = packed[0]
    top_out[4 * DEEP :] = packed[1]


def bond_sum(dx, own, words, far, total, rows=range(-HORIZON, HORIZON + 1)):
    from_x = own[0] - float(dx)
    from_z = {dz: own[2] - float(dz) for dz in range(-HORIZON, HORIZON + 1)}
    for dy in rows:
        from_y = own[1] - float(dy)
        for dz in range(-HORIZON, HORIZON + 1):
            if (dx, dy, dz) not in BONDS:
                continue
            radius = float(dx * dx + dy * dy + dz * dz)
            word, bit = BONDS[dx, dy, dz]
            there = far(dy, dz)
            stretch_x = there[0] - from_x
            stretch_y = there[1] - from_y
            stretch_z = there[2] - from_z[dz]
            inverse = lax.rsqrt(stretch_x * stretch_x + stretch_y * stretch_y + stretch_z * stretch_z)
            factor = (BOND_SCALE / radius - (BOND_SCALE / radius**0.5) * inverse) * there[3]
            factor = jnp.where((words(word) & (1 << bit)) == 0, factor, 0.0)
            total = (
                total[0] + factor * stretch_x,
                total[1] + factor * stretch_y,
                total[2] + factor * stretch_z,
            )
    return total


SHIFTS = (-2, -1, 1, 2)


def inner_sum(x, rows, bits, own, total, field_rows, near, far):
    def words(word):
        return bits[word, x]

    for dx in (0, -1, 1, -2, 2, -3, 3):
        if 0 <= x + dx < 8:

            def there(dy, dz, dx=dx):
                if dz == 0:
                    return [field_rows(field, x + dx, dy) for field in range(4)]
                if abs(dz) == 3:
                    return [far[int(dz > 0), field, x + dx] for field in range(4)]
                rows = slice(OWN + dy, OWN + dy + 8)
                return [near[SHIFTS.index(dz), field, x + dx, rows] for field in range(4)]

            total = bond_sum(dx, own, words, there, total, rows)
    return total


def first_kernel(wide, main, side, bits, fields, partial_out, near_out, frame_out, next_out, far, sem):
    copy = pltpu.make_async_copy(fields.at[:3], next_out, sem)
    copy.start()
    own_rows = slice(OWN, OWN + 8)
    for field in range(4):
        for x in range(8):
            block = main[field, x]
            margin = side[field, x] if wide else None
            frame_out[field, x, own_rows] = block
            for slot, dz in enumerate(SHIFTS):
                near_out[slot, field, x, own_rows] = z_window(block, margin, dz, wide)
            for slot, dz in enumerate((-3, 3)):
                far[slot, field, x] = z_window(block, margin, dz, wide)
    for x in range(8):
        own = [main[field, x] for field in range(3)]
        total = (jnp.zeros((8, LANES), jnp.float32),) * 3

        def field_rows(field, layer, dy):
            return main[field, layer]

        total = inner_sum(x, (0,), bits, own, total, field_rows, near_out, far)
        for field in range(3):
            partial_out[field, x] = total[field]
    copy.wait()


def second_kernel(wide, below, above, bits, partial, near, frame, partial_out, near_out, frame_out, hold):
    for face, block in enumerate((below, above)):
        for field in range(4):
            for group in range(3):
                row = RIM * field + 8 * group
                rows = block[row : row + 8]
                margin = unpack_margins(block[4 * RIM :], field, group) if wide else None
                for slot, dz in enumerate(SHIFTS):
                    hold[face, slot, field, 8 * group : 8 * group + 8] = z_window(rows, margin, dz, wide)
    for field in range(4):
        for x in range(8):
            row = RIM * field + 3 * x
            frame_out[field, x, 1:OWN] = below[row : row + 3]
            frame_out[field, x, OWN + 8 : 15] = above[row : row + 3]
            for slot in range(4):
                near_out[slot, field, x, 2:OWN] = hold[0, slot, field, 3 * x + 1 : 3 * x + 3]
                near_out[slot, field, x, OWN + 8 : 14] = hold[1, slot, field, 3 * x : 3 * x + 2]
    for x in range(8):
        own = [frame_out[field, x, OWN : OWN + 8] for field in range(3)]
        total = tuple(partial[field, x] for field in range(3))

        def field_rows(field, layer, dy):
            return frame_out[field, layer, OWN + dy : OWN + dy + 8]

        total = inner_sum(x, (-3, -2, -1, 1, 2, 3), bits, own, total, field_rows, near_out, None)
        for field in range(3):
            partial_out[field, x] = total[field]


def outer_kernel(
    wide, fields, below, above, bits, vel, partial, force_out, vel_out, layer, near, hold, force_buf, vel_buf, sem
):
    copies = []

    def finish(x, total, root):
        for field in range(3):
            force = root * total[field]
            force_buf[x, field] = force
            vel_buf[x, field] = vel[field, x] + DT_STEP * force
        for slot, (buf, out) in enumerate(((force_buf, force_out), (vel_buf, vel_out))):
            copies.append(pltpu.make_async_copy(buf.at[x], out.at[:, x], sem.at[slot, x]))
            copies[-1].start()

    for x in (3, 4):
        finish(x, [partial[field, x] for field in range(3)], fields[3, x])
    for face, block in enumerate((below, above)):
        for field in range(4):
            row = DEEP * field
            layer[face, 0, field, 2:14] = block[row : row + 12]
            layer[face, 1, field, 2:14] = block[row + 12 : row + 24]
            if wide:
                for group in range(3):
                    rows = slice(8 * group, 8 * group + 8)
                    hold[0, rows] = unpack_margins(block[4 * DEEP :], field, group)
                hold[1, 2:14] = hold[0, :12]
                hold[2, 2:14] = hold[0, 12:24]
            for depth in range(2):
                for half in range(2):
                    rows = slice(8 * half, 8 * half + 8)
                    inner = layer[face, depth, field, rows]
                    margin = hold[1 + depth, rows] if wide else None
                    for slot, dz in enumerate(SHIFTS):
                        near[face, depth, slot, field, rows] = z_window(inner, margin, dz, wide)
    for x in (2, 5, 1, 6, 0, 7):
        total = tuple(partial[field, x] for field in range(3))
        own = [fields[field, x] for field in range(4)]
        for dx in range(-HORIZON, HORIZON + 1):
            if 0 <= x + dx < 8:
                continue
            face = 0 if dx < 0 else 1
            depth = -(x + dx) - 1 if dx < 0 else x + dx - 8
            block = below if dx < 0 else above

            def there(dy, dz, face=face, depth=depth, block=block):
                rows = slice(OWN + dy, OWN + dy + 8)
                if depth == 2:
                    return [block[DEEP * field + 24 : DEEP * field + 32] for field in range(4)]
                if dz == 0:
                    return [layer[face, depth, field, rows] for field in range(4)]
                slot = SHIFTS.index(dz)
                return [near[face, depth, slot, field, rows] for field in range(4)]

            total = bond_sum(dx, own, lambda word, x=x: bits[word, x], there, total)
        finish(x, total, own[3])
    for copy in copies:
        copy.wait()


VMEM = pl.BlockSpec(memory_space=pltpu.VMEM)
HBM = pl.BlockSpec(memory_space=pltpu.HBM)


def call(kernel, ins, outs, scratch, flops, *operands, aliases=()):
    shapes = [jax.ShapeDtypeStruct(shape, jnp.float32) for shape, _ in outs]
    moved = sum(4 * int(a.size) for a in operands) + sum(4 * int(a.size) for a in shapes)
    return pl.pallas_call(
        kernel,
        out_shape=shapes,
        in_specs=ins,
        out_specs=[place for _, place in outs],
        scratch_shapes=[pltpu.VMEM(a, jnp.float32) if isinstance(a, tuple) else a for a in scratch],
        input_output_aliases=dict(aliases),
        compiler_params=pltpu.CompilerParams(vmem_limit_bytes=24 * 1024 * 1024),
        cost_estimate=pl.CostEstimate(flops=flops, bytes_accessed=moved, transcendentals=0),
    )(*operands)


Y_TURNED = False
X_TURNED = True


def traded(low, top, axis, turned):
    count = lax.axis_size(axis)
    even = lax.axis_index(axis) % 2 == 0
    got = []
    for start, block in ((0, jnp.where(even, top, low)), (1, jnp.where(even, low, top))):
        pairs = []
        for i in range(start, count - 1, 2):
            pairs += [(i, i + 1), (i + 1, i)]
        got.append(lax.ppermute(block, axis, pairs) if pairs else jnp.zeros_like(block))
    if turned:
        outer, middle = lax.optimization_barrier((got[0], got[1]))
    else:
        middle, outer = lax.optimization_barrier((got[1], got[0]))
    return jnp.where(even, middle, outer), jnp.where(even, outer, middle)


def body(displacement, velocity, micromodulus, damage_bits):
    cells_z = micromodulus.shape[2]
    wide = cells_z == LANES
    if not wide:
        pad = [(0, 0), (0, 0), (0, 0), (0, LANES - cells_z)]
        displacement, velocity, damage_bits = (
            jnp.pad(a, pad) for a in (displacement, velocity, damage_bits)
        )
        micromodulus = jnp.pad(micromodulus, pad[1:])
    brick = (8, 8, LANES)
    fields, kept, z_msg = call(
        functools.partial(advance_kernel, cells_z),
        [HBM] * 3,
        [((4, *brick), VMEM), ((3, *brick), VMEM), ((4, 8, LANES), VMEM)],
        [(3, *brick), brick, pltpu.SemaphoreType.DMA((3,))],
        100_000,
        *(pltpu.with_memory_space_constraint(a, pltpu.HBM) for a in (displacement, velocity, micromodulus)),
    )
    first_half = lax.broadcasted_iota(jnp.int32, z_msg.shape, 2) < 64
    count = lax.axis_size("gz")
    place = lax.axis_index("gz")
    if count == 2:
        other = lax.ppermute(z_msg, "gz", [(0, 1), (1, 0)])
        z_got = jnp.where(first_half == (place == 1), other, 0.0)
    else:
        before, after = traded(z_msg, z_msg, "gz", False)
        z_got = jnp.where(first_half, before, after)
    rim_msg = ((4 * RIM + 8, LANES), VMEM)
    main, side, low, top = call(
        functools.partial(side_kernel, cells_z),
        [VMEM] * 2,
        [((4, *brick), VMEM), ((4, *brick), VMEM), rim_msg, rim_msg],
        [(2, RIM, LANES)],
        100_000,
        fields,
        z_got,
    )
    below, above = traded(low, top, "gy", Y_TURNED)
    near = ((4, 4, 8, FRAME, LANES), VMEM)
    framed = ((4, 8, FRAME, LANES), VMEM)
    partial, windows, frame, advanced = call(
        functools.partial(first_kernel, wide),
        [VMEM] * 4,
        [((3, *brick), VMEM), near, framed, ((3, *brick), HBM)],
        [(2, 4, *brick), pltpu.SemaphoreType.DMA],
        5_000_000,
        main,
        side,
        damage_bits,
        fields,
    )
    below, above, partial = lax.optimization_barrier((below, above, partial))
    deep_msg = ((4 * DEEP + 8, LANES), VMEM)
    low, top = call(
        functools.partial(deep_kernel, wide),
        [VMEM] * 4,
        [deep_msg, deep_msg],
        [(4, RIM, LANES)],
        100_000,
        main,
        side,
        below,
        above,
    )
    rim_below, rim_above = below, above
    below, above = traded(low, top, "gx", X_TURNED)
    partial, _, _ = call(
        functools.partial(second_kernel, wide),
        [VMEM] * 6,
        [((3, *brick), VMEM), near, framed],
        [(2, 4, 4, RIM, LANES)],
        20_000_000,
        rim_below,
        rim_above,
        damage_bits,
        partial,
        windows,
        frame,
        aliases=((4, 1), (5, 2)),
    )
    force, moved = call(
        functools.partial(outer_kernel, wide),
        [VMEM] * 6,
        [((3, *brick), HBM), ((3, *brick), HBM)],
        [
            (2, 2, 4, FRAME, LANES),
            (2, 2, 4, 4, FRAME, LANES),
            (3, RIM, LANES),
            (8, 3, 8, LANES),
            (8, 3, 8, LANES),
            pltpu.SemaphoreType.DMA((2, 8)),
        ],
        4_000_000,
        fields,
        below,
        above,
        damage_bits,
        kept,
        partial,
    )
    return force[..., :cells_z], advanced[..., :cells_z], moved[..., :cells_z]


def solution(mesh):
    placed = P(None, "gx", "gy", "gz")
    return jax.shard_map(
        body,
        mesh=mesh,
        in_specs=(placed, placed, P("gx", "gy", "gz"), placed),
        out_specs=(placed, placed, placed),
        check_vma=False,
    )
```

```python
import functools

import jax
import jax.numpy as jnp
from jax import lax
from jax.experimental import pallas as pl
from jax.experimental.pallas import tpu as pltpu
from jax.sharding import PartitionSpec as P

HORIZON = 3
DT_STEP = 0.25
BOND_SCALE = 5.0
LANES = 128
ROWS = 64
FRAME = 16
OWN = 4
CORE = slice(OWN, OWN + 8)
RIM = 24
DEEP = 32
SHIFTS = (-2, -1, 1, 2)
REACH = range(-HORIZON, HORIZON + 1)


def bond_table():
    table = {}
    number = 0
    for dx in REACH:
        for dy in REACH:
            for dz in REACH:
                radius = dx * dx + dy * dy + dz * dz
                if 0 < radius <= HORIZON * HORIZON and (dx, dy, dz) > (0, 0, 0):
                    table[dx, dy, dz] = (number // 12, number % 12)
                    table[-dx, -dy, -dz] = (6 + number // 12, number % 12)
                    number += 1
    return table


BONDS = bond_table()


def lane_ids():
    return lax.broadcasted_iota(jnp.int32, (8, LANES), 1)


def nothing():
    return jnp.zeros((8, LANES), jnp.float32)


def layer_rows(x):
    return slice(8 * x, 8 * x + 8)


def across(y):
    return pl.ds(y, 8, stride=8)


def rolled(block, shift):
    shift = shift % LANES
    return pltpu.roll(block, shift, axis=1) if shift else block


def z_window(main, side, dz, wide):
    if not wide:
        return rolled(main, -dz)
    lane = lane_ids()
    if dz > 0:
        return rolled(jnp.where(lane < dz, side, main), -dz)
    return rolled(jnp.where(lane >= LANES + dz, side, main), -dz)


def pack_margins(packed, rows, field, group):
    lane = lane_ids()
    start = 4 * (3 * field + group)
    return jnp.where((lane >= start) & (lane < start + 4), rolled(rows, 2 + start), packed)


def unpack_margins(packed, field, group):
    lane = lane_ids()
    return jnp.where((lane >= 126) | (lane < 2), rolled(packed, -(2 + 4 * (3 * field + group))), 0.0)


def bond_sum(offsets, own, words, far, total):
    bases = {}

    def base(axis, step):
        if (axis, step) not in bases:
            bases[axis, step] = own[axis] - float(step) if step else own[axis]
        return bases[axis, step]

    for offset in offsets:
        radius = float(sum(step * step for step in offset))
        word, bit = BONDS[offset]
        there = far(offset)
        stretch = [there[axis] - base(axis, offset[axis]) for axis in range(3)]
        inverse = lax.rsqrt(stretch[0] * stretch[0] + stretch[1] * stretch[1] + stretch[2] * stretch[2])
        factor = (BOND_SCALE / radius - (BOND_SCALE / radius**0.5) * inverse) * there[3]
        factor = jnp.where((words(word) & (1 << bit)) == 0, factor, 0.0)
        total = tuple(total[axis] + factor * stretch[axis] for axis in range(3))
    return total


def advance_kernel(cells_z, disp, vel, mod, field_out, vel_out, msg_out, hold, hold_mod, sem):
    copies = [
        pltpu.make_async_copy(disp, hold, sem.at[0]),
        pltpu.make_async_copy(vel, vel_out, sem.at[1]),
        pltpu.make_async_copy(mod, hold_mod, sem.at[2]),
    ]
    for copy in copies:
        copy.start()
    for copy in copies:
        copy.wait()
    lane = lane_ids()
    for field in range(4):
        packed = nothing()
        for x in range(8):
            rows = layer_rows(x)
            if field < 3:
                own = hold[field, rows] + DT_STEP * vel_out[field, rows]
            else:
                own = jnp.sqrt(hold_mod[rows])
            field_out[field, rows] = own
            top = rolled(own, 8 * x - (cells_z - 3))
            low = rolled(own, 64 + 8 * x)
            packed = jnp.where((lane >= 8 * x) & (lane < 8 * x + 3), top, packed)
            packed = jnp.where((lane >= 64 + 8 * x) & (lane < 64 + 8 * x + 3), low, packed)
        msg_out[field] = packed


def side_kernel(cells_z, fields, arrived, main_out, side_out, low_out, top_out):
    wide = cells_z == LANES
    lane = lane_ids()
    first = cells_z % LANES
    packed = [nothing(), nothing()]
    for field in range(4):
        got = arrived[field]
        for x in range(8):
            rows = layer_rows(x)
            own = fields[field, rows]
            below = rolled(got, 125 - 8 * x)
            above = rolled(got, first - (64 + 8 * x))
            side = jnp.where((lane >= first) & (lane < first + 3), above, 0.0)
            side = jnp.where(lane >= 125, below, side)
            if not wide:
                own = jnp.where(lane < cells_z, own, side)
            main_out[field, rows] = own
            side_out[field, rows] = side
        for face, out in enumerate((low_out, top_out)):
            for r in range(3):
                y = 5 * face + r
                out[RIM * field + 8 * r : RIM * field + 8 * r + 8] = main_out[field, across(y)]
                if wide:
                    packed[face] = pack_margins(packed[face], side_out[field, across(y)], field, r)
    low_out[4 * RIM :] = packed[0]
    top_out[4 * RIM :] = packed[1]


def inside_kernel(wide, main, side, bits, fields, partial_out, next_out, frame, near, far, sem):
    copy = pltpu.make_async_copy(fields.at[:3], next_out, sem)
    copy.start()
    blank = jnp.zeros((OWN, LANES), jnp.float32)
    for field in range(4):
        for x in range(8):
            block = main[field, layer_rows(x)]
            margin = side[field, layer_rows(x)] if wide else None
            frame[field, x, :OWN] = blank
            frame[field, x, OWN + 8 :] = blank
            frame[field, x, CORE] = block
            for slot, dz in enumerate(SHIFTS):
                near[slot, field, x, :OWN] = blank
                near[slot, field, x, OWN + 8 :] = blank
                near[slot, field, x, CORE] = z_window(block, margin, dz, wide)
            for slot, dz in enumerate((-3, 3)):
                far[slot, field, x] = z_window(block, margin, dz, wide)
    for x in range(8):

        def there(offset, x=x):
            dx, dy, dz = offset
            rows = slice(OWN + dy, OWN + dy + 8)
            if dz == 0:
                return [frame[field, x + dx, rows] for field in range(4)]
            if abs(dz) == 3:
                return [far[int(dz > 0), field, x + dx] for field in range(4)]
            return [near[SHIFTS.index(dz), field, x + dx, rows] for field in range(4)]

        rows = layer_rows(x)
        own = [main[field, rows] for field in range(3)]
        offsets = [offset for offset in BONDS if 0 <= x + offset[0] < 8]
        total = bond_sum(offsets, own, lambda word, rows=rows: bits[word, rows], there, (nothing(),) * 3)
        for axis in range(3):
            partial_out[axis, rows] = total[axis]
    copy.wait()


def deep_kernel(wide, main, side, below, above, low_out, top_out, hold):
    packed = [nothing(), nothing()]
    sources = ((below, 1, 0), (below, 2, 0), (above, 0, 1), (above, 1, 1))
    for field in range(4):
        if wide:
            for face, block in enumerate((below, above)):
                for r in range(3):
                    hold[face, 8 * r : 8 * r + 8] = unpack_margins(block[4 * RIM :], field, r)
        for face, (out, layers) in enumerate(((low_out, (0, 1, 2)), (top_out, (7, 6, 5)))):
            start = DEEP * field
            for depth, x in enumerate(layers):
                out[start + 8 * depth : start + 8 * depth + 8] = main[field, layer_rows(x)]
                if depth == 2:
                    continue
                for place, (block, r, source) in enumerate(sources):
                    row = 4 * depth + place
                    rim = RIM * field + 8 * r + x
                    out[start + 24 + row : start + 25 + row] = block[rim : rim + 1]
                    if wide:
                        hold[2 + face, row : row + 1] = hold[source, 8 * r + x : 8 * r + x + 1]
            if wide:
                for group, x in enumerate(layers[:2]):
                    packed[face] = pack_margins(packed[face], side[field, layer_rows(x)], field, group)
                packed[face] = pack_margins(packed[face], hold[2 + face, :8], field, 2)
    low_out[4 * DEEP :] = packed[0]
    top_out[4 * DEEP :] = packed[1]


def rim_kernel(wide, main, below, above, bits, partial, partial_out, frame, near):
    blank = jnp.zeros((OWN, LANES), jnp.float32)
    for face, block in enumerate((below, above)):
        for field in range(4):
            for r in range(3):
                rows = block[RIM * field + 8 * r : RIM * field + 8 * r + 8]
                height = r + 1 if face else 3 - r
                frame[face, height - 1, field, :OWN] = blank
                frame[face, height - 1, field, CORE] = rows
                frame[face, height - 1, field, OWN + 8 :] = blank
                if height == 3:
                    continue
                margin = unpack_margins(block[4 * RIM :], field, r) if wide else None
                for slot, dz in enumerate(SHIFTS):
                    near[slot, face, height - 1, field, :OWN] = blank
                    near[slot, face, height - 1, field, CORE] = z_window(rows, margin, dz, wide)
                    near[slot, face, height - 1, field, OWN + 8 :] = blank
    for axis in range(3):
        for x in range(8):
            partial_out[axis, layer_rows(x)] = partial[axis, layer_rows(x)]
    for face in range(2):
        for depth in range(3):
            y = 7 - depth if face else depth

            def there(offset, face=face, depth=depth):
                dx, dy, dz = offset
                height = abs(dy) - depth - 1
                rows = slice(OWN + dx, OWN + dx + 8)
                if dz == 0:
                    return [frame[face, height, field, rows] for field in range(4)]
                return [near[SHIFTS.index(dz), face, height, field, rows] for field in range(4)]

            own = [main[field, across(y)] for field in range(3)]
            offsets = [offset for offset in BONDS if not 0 <= y + offset[1] < 8]
            total = tuple(partial_out[axis, across(y)] for axis in range(3))
            total = bond_sum(offsets, own, lambda word, y=y: bits[word, across(y)], there, total)
            for axis in range(3):
                partial_out[axis, across(y)] = total[axis]


def face_layers(face):
    return (7, 6, 5) if face else (0, 1, 2)


def face_windows(wide, block, frame, near):
    for field in range(4):
        start = DEEP * field
        groups = [block[start + 8 * group : start + 8 * group + 8] for group in (0, 1, 3)]
        margins = [unpack_margins(block[4 * DEEP :], field, group) if wide else None for group in range(3)]
        views = [(frame, groups)]
        for slot, dz in enumerate(SHIFTS):
            views.append((near.at[slot], [z_window(*pair, dz, wide) for pair in zip(groups, margins)]))
        for ref, parts in views:
            for depth in range(2):
                ref[depth, field, CORE] = parts[depth]
                ref[depth, field, 2:OWN] = parts[2][4 * depth : 4 * depth + 2]
                ref[depth, field, OWN + 8 : 14] = parts[2][4 * depth + 2 : 4 * depth + 4]


def face_sum(face, x, main, block, bits, frame, near, total):
    def there(offset):
        dx, dy, dz = offset
        depth = x + dx - 8 if face else -(x + dx) - 1
        rows = slice(OWN + dy, OWN + dy + 8)
        if depth == 2:
            return [block[DEEP * field + 16 : DEEP * field + 24] for field in range(4)]
        if dz == 0:
            return [frame[depth, field, rows] for field in range(4)]
        return [near[SHIFTS.index(dz), depth, field, rows] for field in range(4)]

    rows = layer_rows(x)
    own = [main[field, rows] for field in range(3)]
    offsets = [offset for offset in BONDS if not 0 <= x + offset[0] < 8 and (offset[0] > 0) == bool(face)]
    return bond_sum(offsets, own, lambda word: bits[word, rows], there, total)


def first_face_kernel(wide, main, block, bits, partial, partial_out, frame, near):
    for axis in range(3):
        for x in range(8):
            partial_out[axis, layer_rows(x)] = partial[axis, layer_rows(x)]
    face_windows(wide, block, frame, near)
    even = lax.axis_index("gx") % 2 == 0
    for face in range(2):

        @pl.when(even if face else jnp.logical_not(even))
        def _(face=face):
            for x in face_layers(face):
                rows = layer_rows(x)
                total = tuple(partial[axis, rows] for axis in range(3))
                total = face_sum(face, x, main, block, bits, frame, near, total)
                for axis in range(3):
                    partial_out[axis, rows] = total[axis]


def last_face_kernel(
    wide, main, block, bits, vel, partial, force_out, vel_out, frame, near, force_buf, vel_buf, sem
):
    def finish(x, total, copies):
        rows = layer_rows(x)
        root = main[3, rows]
        for axis in range(3):
            force = root * total[axis]
            force_buf[axis, rows] = force
            vel_buf[axis, rows] = vel[axis, rows] + DT_STEP * force
        for slot, (buf, out) in enumerate(((force_buf, force_out), (vel_buf, vel_out))):
            copies.append(pltpu.make_async_copy(buf.at[:, rows], out.at[:, rows], sem.at[slot, x]))
            copies[-1].start()

    even = lax.axis_index("gx") % 2 == 0
    for face in range(2):

        @pl.when(jnp.logical_not(even) if face else even)
        def _(face=face):
            copies = []
            layers = face_layers(face)
            for x in range(8):
                if x not in layers:
                    finish(x, [partial[axis, layer_rows(x)] for axis in range(3)], copies)
            face_windows(wide, block, frame, near)
            for x in layers[::-1]:
                total = tuple(partial[axis, layer_rows(x)] for axis in range(3))
                finish(x, face_sum(face, x, main, block, bits, frame, near, total), copies)
            for copy in copies:
                copy.wait()


VMEM = pl.BlockSpec(memory_space=pltpu.VMEM)
HBM = pl.BlockSpec(memory_space=pltpu.HBM)


def call(kernel, ins, outs, scratch, flops, *operands):
    shapes = [jax.ShapeDtypeStruct(shape, jnp.float32) for shape, _ in outs]
    moved = sum(4 * int(a.size) for a in operands) + sum(4 * int(a.size) for a in shapes)
    return pl.pallas_call(
        kernel,
        out_shape=shapes,
        in_specs=ins,
        out_specs=[place for _, place in outs],
        scratch_shapes=[pltpu.VMEM(a, jnp.float32) if isinstance(a, tuple) else a for a in scratch],
        compiler_params=pltpu.CompilerParams(vmem_limit_bytes=24 * 1024 * 1024),
        cost_estimate=pl.CostEstimate(flops=flops, bytes_accessed=moved, transcendentals=0),
    )(*operands)


def traded(low, top, axis):
    count = lax.axis_size(axis)
    even = lax.axis_index(axis) % 2 == 0
    got = []
    for start, block in ((0, jnp.where(even, top, low)), (1, jnp.where(even, low, top))):
        pairs = []
        for i in range(start, count - 1, 2):
            pairs += [(i, i + 1), (i + 1, i)]
        got.append(lax.ppermute(block, axis, pairs) if pairs else jnp.zeros_like(block))
    return even, got


def body(displacement, velocity, micromodulus, damage_bits):
    cells_z = micromodulus.shape[2]
    wide = cells_z == LANES
    if not wide:
        pad = [(0, 0), (0, 0), (0, 0), (0, LANES - cells_z)]
        displacement, velocity, damage_bits = (
            jnp.pad(a, pad) for a in (displacement, velocity, damage_bits)
        )
        micromodulus = jnp.pad(micromodulus, pad[1:])
    shape = displacement.shape
    displacement = displacement.reshape(3, ROWS, LANES)
    velocity = velocity.reshape(3, ROWS, LANES)
    micromodulus = micromodulus.reshape(ROWS, LANES)
    damage_bits = damage_bits.reshape(12, ROWS, LANES)
    vectors = (3, ROWS, LANES)
    all_fields = (4, ROWS, LANES)
    fields, kept, z_msg = call(
        functools.partial(advance_kernel, cells_z),
        [HBM] * 3,
        [(all_fields, VMEM), (vectors, VMEM), ((4, 8, LANES), VMEM)],
        [vectors, (ROWS, LANES), pltpu.SemaphoreType.DMA((3,))],
        100_000,
        *(pltpu.with_memory_space_constraint(a, pltpu.HBM) for a in (displacement, velocity, micromodulus)),
    )
    first_half = lax.broadcasted_iota(jnp.int32, z_msg.shape, 2) < 64
    place = lax.axis_index("gz")
    if lax.axis_size("gz") == 2:
        other = lax.ppermute(z_msg, "gz", [(0, 1), (1, 0)])
        z_got = jnp.where(first_half == (place == 1), other, 0.0)
    else:
        even, got = traded(z_msg, z_msg, "gz")
        z_got = jnp.where(first_half == even, got[1], got[0])
    rim_msg = ((4 * RIM + 8, LANES), VMEM)
    main, side, low, top = call(
        functools.partial(side_kernel, cells_z),
        [VMEM] * 2,
        [(all_fields, VMEM), (all_fields, VMEM), rim_msg, rim_msg],
        [],
        100_000,
        fields,
        z_got,
    )
    even, got = traded(low, top, "gy")
    partial, advanced = call(
        functools.partial(inside_kernel, wide),
        [VMEM] * 4,
        [(vectors, VMEM), (vectors, HBM)],
        [(4, 8, FRAME, LANES), (4, 4, 8, FRAME, LANES), (2, 4, 8, 8, LANES), pltpu.SemaphoreType.DMA],
        20_000_000,
        main,
        side,
        damage_bits,
        fields,
    )
    outer, inner, partial = lax.optimization_barrier((got[0], got[1], partial))
    below = jnp.where(even, inner, outer)
    above = jnp.where(even, outer, inner)
    deep_msg = ((4 * DEEP + 8, LANES), VMEM)
    low, top = call(
        functools.partial(deep_kernel, wide),
        [VMEM] * 4,
        [deep_msg, deep_msg],
        [(4, RIM, LANES)],
        100_000,
        main,
        side,
        below,
        above,
    )
    even, got = traded(low, top, "gx")
    (partial,) = call(
        functools.partial(rim_kernel, wide),
        [VMEM] * 5,
        [(vectors, VMEM)],
        [(2, 3, 4, FRAME, LANES), (4, 2, 2, 4, FRAME, LANES)],
        4_000_000,
        main,
        below,
        above,
        damage_bits,
        partial,
    )
    windows = [(2, 4, FRAME, LANES), (4, 2, 4, FRAME, LANES)]
    (partial,) = call(
        functools.partial(first_face_kernel, wide),
        [VMEM] * 4,
        [(vectors, VMEM)],
        windows,
        2_000_000,
        main,
        got[0],
        damage_bits,
        partial,
    )
    force, moved = call(
        functools.partial(last_face_kernel, wide),
        [VMEM] * 5,
        [(vectors, HBM), (vectors, HBM)],
        [*windows, vectors, vectors, pltpu.SemaphoreType.DMA((2, 8))],
        2_000_000,
        main,
        got[1],
        damage_bits,
        kept,
        partial,
    )
    return tuple(a.reshape(shape)[..., :cells_z] for a in (force, advanced, moved))


def solution(mesh):
    placed = P(None, "gx", "gy", "gz")
    return jax.shard_map(
        body,
        mesh=mesh,
        in_specs=(placed, placed, P("gx", "gy", "gz"), placed),
        out_specs=(placed, placed, placed),
        check_vma=False,
    )
```

```python
import functools

import jax
import jax.numpy as jnp
from jax import lax
from jax.experimental import pallas as pl
from jax.experimental.pallas import tpu as pltpu
from jax.sharding import PartitionSpec as P

HORIZON = 3
DT_STEP = 0.25
BOND_SCALE = 5.0
LANES = 128
ROWS = 64
FRAME = 16
OWN = 4
CORE = slice(OWN, OWN + 8)
RIM = 24
DEEP = 32
SHIFTS = (-2, -1, 1, 2)
REACH = range(-HORIZON, HORIZON + 1)


def bond_table():
    table = {}
    number = 0
    for dx in REACH:
        for dy in REACH:
            for dz in REACH:
                radius = dx * dx + dy * dy + dz * dz
                if 0 < radius <= HORIZON * HORIZON and (dx, dy, dz) > (0, 0, 0):
                    table[dx, dy, dz] = (number // 12, number % 12)
                    table[-dx, -dy, -dz] = (6 + number // 12, number % 12)
                    number += 1
    return table


BONDS = bond_table()


def lane_ids():
    return lax.broadcasted_iota(jnp.int32, (8, LANES), 1)


def nothing():
    return jnp.zeros((8, LANES), jnp.float32)


def layer_rows(x):
    return slice(8 * x, 8 * x + 8)


def across(y):
    return pl.ds(y, 8, stride=8)


def rolled(block, shift):
    shift = shift % LANES
    return pltpu.roll(block, shift, axis=1) if shift else block


def z_window(main, side, dz, wide):
    if not wide:
        return rolled(main, -dz)
    lane = lane_ids()
    if dz > 0:
        return rolled(jnp.where(lane < dz, side, main), -dz)
    return rolled(jnp.where(lane >= LANES + dz, side, main), -dz)


def pack_margins(packed, rows, field, group):
    lane = lane_ids()
    start = 4 * (3 * field + group)
    return jnp.where((lane >= start) & (lane < start + 4), rolled(rows, 2 + start), packed)


def unpack_margins(packed, field, group):
    lane = lane_ids()
    return jnp.where((lane >= 126) | (lane < 2), rolled(packed, -(2 + 4 * (3 * field + group))), 0.0)


def bond_sum(offsets, own, words, far, total):
    bases = {}

    def base(axis, step):
        if (axis, step) not in bases:
            bases[axis, step] = own[axis] - float(step) if step else own[axis]
        return bases[axis, step]

    for offset in offsets:
        radius = float(sum(step * step for step in offset))
        word, bit = BONDS[offset]
        there = far(offset)
        stretch = [there[axis] - base(axis, offset[axis]) for axis in range(3)]
        inverse = lax.rsqrt(stretch[0] * stretch[0] + stretch[1] * stretch[1] + stretch[2] * stretch[2])
        factor = (BOND_SCALE / radius - (BOND_SCALE / radius**0.5) * inverse) * there[3]
        factor = jnp.where((words(word) & (1 << bit)) == 0, factor, 0.0)
        total = tuple(total[axis] + factor * stretch[axis] for axis in range(3))
    return total


def advance_kernel(cells_z, disp, vel, mod, field_out, vel_out, msg_out, hold, hold_mod, sem):
    copies = [
        pltpu.make_async_copy(disp, hold, sem.at[0]),
        pltpu.make_async_copy(vel, vel_out, sem.at[1]),
        pltpu.make_async_copy(mod, hold_mod, sem.at[2]),
    ]
    for copy in copies:
        copy.start()
    for copy in copies:
        copy.wait()
    lane = lane_ids()
    for field in range(4):
        packed = nothing()
        for x in range(8):
            rows = layer_rows(x)
            if field < 3:
                own = hold[field, rows] + DT_STEP * vel_out[field, rows]
            else:
                own = jnp.sqrt(hold_mod[rows])
            field_out[field, rows] = own
            top = rolled(own, 8 * x - (cells_z - 3))
            low = rolled(own, 64 + 8 * x)
            packed = jnp.where((lane >= 8 * x) & (lane < 8 * x + 3), top, packed)
            packed = jnp.where((lane >= 64 + 8 * x) & (lane < 64 + 8 * x + 3), low, packed)
        msg_out[field] = packed


def side_kernel(cells_z, fields, arrived, main_out, side_out, low_out, top_out):
    wide = cells_z == LANES
    lane = lane_ids()
    first = cells_z % LANES
    packed = [nothing(), nothing()]
    for field in range(4):
        got = arrived[field]
        for x in range(8):
            rows = layer_rows(x)
            own = fields[field, rows]
            below = rolled(got, 125 - 8 * x)
            above = rolled(got, first - (64 + 8 * x))
            side = jnp.where((lane >= first) & (lane < first + 3), above, 0.0)
            side = jnp.where(lane >= 125, below, side)
            if not wide:
                own = jnp.where(lane < cells_z, own, side)
            main_out[field, rows] = own
            side_out[field, rows] = side
        for face, out in enumerate((low_out, top_out)):
            for r in range(3):
                y = 5 * face + r
                out[RIM * field + 8 * r : RIM * field + 8 * r + 8] = main_out[field, across(y)]
                if wide:
                    packed[face] = pack_margins(packed[face], side_out[field, across(y)], field, r)
    low_out[4 * RIM :] = packed[0]
    top_out[4 * RIM :] = packed[1]


def inside_kernel(wide, main, side, bits, fields, partial_out, next_out, frame, near, far, sem):
    copy = pltpu.make_async_copy(fields.at[:3], next_out, sem)
    copy.start()
    blank = jnp.zeros((OWN, LANES), jnp.float32)
    for field in range(4):
        for x in range(8):
            block = main[field, layer_rows(x)]
            margin = side[field, layer_rows(x)] if wide else None
            frame[field, x, :OWN] = blank
            frame[field, x, OWN + 8 :] = blank
            frame[field, x, CORE] = block
            for slot, dz in enumerate(SHIFTS):
                near[slot, field, x, :OWN] = blank
                near[slot, field, x, OWN + 8 :] = blank
                near[slot, field, x, CORE] = z_window(block, margin, dz, wide)
            for slot, dz in enumerate((-3, 3)):
                far[slot, field, x] = z_window(block, margin, dz, wide)
    for x in range(8):

        def there(offset, x=x):
            dx, dy, dz = offset
            rows = slice(OWN + dy, OWN + dy + 8)
            if dz == 0:
                return [frame[field, x + dx, rows] for field in range(4)]
            if abs(dz) == 3:
                return [far[int(dz > 0), field, x + dx] for field in range(4)]
            return [near[SHIFTS.index(dz), field, x + dx, rows] for field in range(4)]

        rows = layer_rows(x)
        own = [main[field, rows] for field in range(3)]
        offsets = [offset for offset in BONDS if 0 <= x + offset[0] < 8]
        total = bond_sum(offsets, own, lambda word, rows=rows: bits[word, rows], there, (nothing(),) * 3)
        for axis in range(3):
            partial_out[axis, rows] = total[axis]
    copy.wait()


def deep_kernel(wide, main, side, below, above, low_out, top_out, hold):
    packed = [nothing(), nothing()]
    sources = ((below, 1, 0), (below, 2, 0), (above, 0, 1), (above, 1, 1))
    for field in range(4):
        if wide:
            for face, block in enumerate((below, above)):
                for r in range(3):
                    hold[face, 8 * r : 8 * r + 8] = unpack_margins(block[4 * RIM :], field, r)
        for face, (out, layers) in enumerate(((low_out, (0, 1, 2)), (top_out, (7, 6, 5)))):
            start = DEEP * field
            for depth, x in enumerate(layers):
                out[start + 8 * depth : start + 8 * depth + 8] = main[field, layer_rows(x)]
                if depth == 2:
                    continue
                for place, (block, r, source) in enumerate(sources):
                    row = 4 * depth + place
                    rim = RIM * field + 8 * r + x
                    out[start + 24 + row : start + 25 + row] = block[rim : rim + 1]
                    if wide:
                        hold[2 + face, row : row + 1] = hold[source, 8 * r + x : 8 * r + x + 1]
            if wide:
                for group, x in enumerate(layers[:2]):
                    packed[face] = pack_margins(packed[face], side[field, layer_rows(x)], field, group)
                packed[face] = pack_margins(packed[face], hold[2 + face, :8], field, 2)
    low_out[4 * DEEP :] = packed[0]
    top_out[4 * DEEP :] = packed[1]


def rim_kernel(wide, main, below, above, bits, partial, partial_out, frame, near):
    blank = jnp.zeros((OWN, LANES), jnp.float32)
    for face, block in enumerate((below, above)):
        for field in range(4):
            for r in range(3):
                rows = block[RIM * field + 8 * r : RIM * field + 8 * r + 8]
                height = r + 1 if face else 3 - r
                frame[face, height - 1, field, :OWN] = blank
                frame[face, height - 1, field, CORE] = rows
                frame[face, height - 1, field, OWN + 8 :] = blank
                if height == 3:
                    continue
                margin = unpack_margins(block[4 * RIM :], field, r) if wide else None
                for slot, dz in enumerate(SHIFTS):
                    near[slot, face, height - 1, field, :OWN] = blank
                    near[slot, face, height - 1, field, CORE] = z_window(rows, margin, dz, wide)
                    near[slot, face, height - 1, field, OWN + 8 :] = blank
    for axis in range(3):
        for x in range(8):
            partial_out[axis, layer_rows(x)] = partial[axis, layer_rows(x)]
    for face in range(2):
        for depth in range(3):
            y = 7 - depth if face else depth

            def there(offset, face=face, depth=depth):
                dx, dy, dz = offset
                height = abs(dy) - depth - 1
                rows = slice(OWN + dx, OWN + dx + 8)
                if dz == 0:
                    return [frame[face, height, field, rows] for field in range(4)]
                return [near[SHIFTS.index(dz), face, height, field, rows] for field in range(4)]

            own = [main[field, across(y)] for field in range(3)]
            offsets = [offset for offset in BONDS if not 0 <= y + offset[1] < 8]
            total = tuple(partial_out[axis, across(y)] for axis in range(3))
            total = bond_sum(offsets, own, lambda word, y=y: bits[word, across(y)], there, total)
            for axis in range(3):
                partial_out[axis, across(y)] = total[axis]


def face_layers(face):
    return (7, 6, 5) if face else (0, 1, 2)


def face_windows(wide, block, frame, near):
    for field in range(4):
        start = DEEP * field
        groups = [block[start + 8 * group : start + 8 * group + 8] for group in (0, 1, 3)]
        margins = [unpack_margins(block[4 * DEEP :], field, group) if wide else None for group in range(3)]
        views = [(frame, groups)]
        for slot, dz in enumerate(SHIFTS):
            views.append((near.at[slot], [z_window(*pair, dz, wide) for pair in zip(groups, margins)]))
        for ref, parts in views:
            for depth in range(2):
                ref[depth, field, CORE] = parts[depth]
                ref[depth, field, 2:OWN] = parts[2][4 * depth : 4 * depth + 2]
                ref[depth, field, OWN + 8 : 14] = parts[2][4 * depth + 2 : 4 * depth + 4]


def face_sum(face, x, main, block, bits, frame, near, total):
    def there(offset):
        dx, dy, dz = offset
        depth = x + dx - 8 if face else -(x + dx) - 1
        rows = slice(OWN + dy, OWN + dy + 8)
        if depth == 2:
            return [block[DEEP * field + 16 : DEEP * field + 24] for field in range(4)]
        if dz == 0:
            return [frame[depth, field, rows] for field in range(4)]
        return [near[SHIFTS.index(dz), depth, field, rows] for field in range(4)]

    rows = layer_rows(x)
    own = [main[field, rows] for field in range(3)]
    offsets = [offset for offset in BONDS if not 0 <= x + offset[0] < 8 and (offset[0] > 0) == bool(face)]
    return bond_sum(offsets, own, lambda word: bits[word, rows], there, total)


def first_face_kernel(wide, main, block, bits, partial, partial_out, frame, near):
    for axis in range(3):
        for x in range(8):
            partial_out[axis, layer_rows(x)] = partial[axis, layer_rows(x)]
    even = lax.axis_index("gx") % 2 == 0
    joined = partnered("gx", 0)
    for face in range(2):

        @pl.when(jnp.logical_and(joined, even if face else jnp.logical_not(even)))
        def _(face=face):
            face_windows(wide, block, frame, near)
            for x in face_layers(face):
                rows = layer_rows(x)
                total = tuple(partial[axis, rows] for axis in range(3))
                total = face_sum(face, x, main, block, bits, frame, near, total)
                for axis in range(3):
                    partial_out[axis, rows] = total[axis]


def last_face_kernel(
    wide, main, block, bits, vel, partial, force_out, vel_out, frame, near, force_buf, vel_buf, sem
):
    def finish(x, total, copies):
        rows = layer_rows(x)
        root = main[3, rows]
        for axis in range(3):
            force = root * total[axis]
            force_buf[axis, rows] = force
            vel_buf[axis, rows] = vel[axis, rows] + DT_STEP * force
        for slot, (buf, out) in enumerate(((force_buf, force_out), (vel_buf, vel_out))):
            copies.append(pltpu.make_async_copy(buf.at[:, rows], out.at[:, rows], sem.at[slot, x]))
            copies[-1].start()

    even = lax.axis_index("gx") % 2 == 0
    joined = partnered("gx", 1)

    @pl.when(jnp.logical_not(joined))
    def _():
        copies = []
        for x in range(8):
            finish(x, [partial[axis, layer_rows(x)] for axis in range(3)], copies)
        for copy in copies:
            copy.wait()

    for face in range(2):

        @pl.when(jnp.logical_and(joined, jnp.logical_not(even) if face else even))
        def _(face=face):
            copies = []
            layers = face_layers(face)
            for x in range(8):
                if x not in layers:
                    finish(x, [partial[axis, layer_rows(x)] for axis in range(3)], copies)
            face_windows(wide, block, frame, near)
            for x in layers[::-1]:
                total = tuple(partial[axis, layer_rows(x)] for axis in range(3))
                finish(x, face_sum(face, x, main, block, bits, frame, near, total), copies)
            for copy in copies:
                copy.wait()


VMEM = pl.BlockSpec(memory_space=pltpu.VMEM)
HBM = pl.BlockSpec(memory_space=pltpu.HBM)


def call(kernel, ins, outs, scratch, flops, *operands):
    shapes = [jax.ShapeDtypeStruct(shape, jnp.float32) for shape, _ in outs]
    moved = sum(4 * int(a.size) for a in operands) + sum(4 * int(a.size) for a in shapes)
    return pl.pallas_call(
        kernel,
        out_shape=shapes,
        in_specs=ins,
        out_specs=[place for _, place in outs],
        scratch_shapes=[pltpu.VMEM(a, jnp.float32) if isinstance(a, tuple) else a for a in scratch],
        compiler_params=pltpu.CompilerParams(vmem_limit_bytes=24 * 1024 * 1024),
        cost_estimate=pl.CostEstimate(flops=flops, bytes_accessed=moved, transcendentals=0),
    )(*operands)


AXES = ("gx", "gy", "gz")


def partnered(axis, start):
    place = lax.axis_index(axis)
    last = start + (lax.axis_size(axis) - start) // 2 * 2
    return jnp.logical_and(place >= start, place < last)


def pairs_of(axis, start):
    sizes = [lax.axis_size(name) for name in AXES]
    which = AXES.index(axis)
    last = start + (sizes[which] - start) // 2 * 2
    stride = 1
    for size in sizes[which + 1 :]:
        stride *= size
    pairs = []
    for device in range(sizes[0] * sizes[1] * sizes[2]):
        place = device // stride % sizes[which]
        if start <= place < last:
            pairs.append((device, device - stride if (place - start) % 2 else device + stride))
        elif axis != "gz" and sizes[2] % 2 == 0:
            pairs.append((device, device ^ 1))
    return pairs


def traded(low, top, axis):
    even = lax.axis_index(axis) % 2 == 0
    blocks = jnp.where(even, top, low), jnp.where(even, low, top)
    return even, [lax.ppermute(block, AXES, pairs_of(axis, start)) for start, block in enumerate(blocks)]


def body(displacement, velocity, micromodulus, damage_bits):
    cells_z = micromodulus.shape[2]
    wide = cells_z == LANES
    if not wide:
        pad = [(0, 0), (0, 0), (0, 0), (0, LANES - cells_z)]
        displacement, velocity, damage_bits = (
            jnp.pad(a, pad) for a in (displacement, velocity, damage_bits)
        )
        micromodulus = jnp.pad(micromodulus, pad[1:])
    shape = displacement.shape
    displacement = displacement.reshape(3, ROWS, LANES)
    velocity = velocity.reshape(3, ROWS, LANES)
    micromodulus = micromodulus.reshape(ROWS, LANES)
    damage_bits = damage_bits.reshape(12, ROWS, LANES)
    vectors = (3, ROWS, LANES)
    all_fields = (4, ROWS, LANES)
    fields, kept, z_msg = call(
        functools.partial(advance_kernel, cells_z),
        [HBM] * 3,
        [(all_fields, VMEM), (vectors, VMEM), ((4, 8, LANES), VMEM)],
        [vectors, (ROWS, LANES), pltpu.SemaphoreType.DMA((3,))],
        100_000,
        *(pltpu.with_memory_space_constraint(a, pltpu.HBM) for a in (displacement, velocity, micromodulus)),
    )
    first_half = lax.broadcasted_iota(jnp.int32, z_msg.shape, 2) < 64
    place = lax.axis_index("gz")
    if lax.axis_size("gz") == 2:
        other = lax.ppermute(z_msg, "gz", [(0, 1), (1, 0)])
        z_got = jnp.where(first_half == (place == 1), other, 0.0)
    else:
        even, got = traded(z_msg, z_msg, "gz")
        got = [jnp.where(partnered("gz", start), a, 0.0) for start, a in enumerate(got)]
        z_got = jnp.where(first_half == even, got[1], got[0])
    rim_msg = ((4 * RIM + 8, LANES), VMEM)
    main, side, low, top = call(
        functools.partial(side_kernel, cells_z),
        [VMEM] * 2,
        [(all_fields, VMEM), (all_fields, VMEM), rim_msg, rim_msg],
        [],
        100_000,
        fields,
        z_got,
    )
    even, got = traded(low, top, "gy")
    partial, advanced = call(
        functools.partial(inside_kernel, wide),
        [VMEM] * 4,
        [(vectors, VMEM), (vectors, HBM)],
        [(4, 8, FRAME, LANES), (4, 4, 8, FRAME, LANES), (2, 4, 8, 8, LANES), pltpu.SemaphoreType.DMA],
        20_000_000,
        main,
        side,
        damage_bits,
        fields,
    )
    outer, inner, partial = lax.optimization_barrier((got[0], got[1], partial))
    outer = jnp.where(partnered("gy", 0), outer, 0.0)
    inner = jnp.where(partnered("gy", 1), inner, 0.0)
    below = jnp.where(even, inner, outer)
    above = jnp.where(even, outer, inner)
    deep_msg = ((4 * DEEP + 8, LANES), VMEM)
    low, top = call(
        functools.partial(deep_kernel, wide),
        [VMEM] * 4,
        [deep_msg, deep_msg],
        [(4, RIM, LANES)],
        100_000,
        main,
        side,
        below,
        above,
    )
    even, got = traded(low, top, "gx")
    (partial,) = call(
        functools.partial(rim_kernel, wide),
        [VMEM] * 5,
        [(vectors, VMEM)],
        [(2, 3, 4, FRAME, LANES), (4, 2, 2, 4, FRAME, LANES)],
        4_000_000,
        main,
        below,
        above,
        damage_bits,
        partial,
    )
    windows = [(2, 4, FRAME, LANES), (4, 2, 4, FRAME, LANES)]
    (partial,) = call(
        functools.partial(first_face_kernel, wide),
        [VMEM] * 4,
        [(vectors, VMEM)],
        windows,
        2_000_000,
        main,
        got[0],
        damage_bits,
        partial,
    )
    force, moved = call(
        functools.partial(last_face_kernel, wide),
        [VMEM] * 5,
        [(vectors, HBM), (vectors, HBM)],
        [*windows, vectors, vectors, pltpu.SemaphoreType.DMA((2, 8))],
        2_000_000,
        main,
        got[1],
        damage_bits,
        kept,
        partial,
    )
    return tuple(a.reshape(shape)[..., :cells_z] for a in (force, advanced, moved))


def solution(mesh):
    placed = P(None, "gx", "gy", "gz")
    return jax.shard_map(
        body,
        mesh=mesh,
        in_specs=(placed, placed, P("gx", "gy", "gz"), placed),
        out_specs=(placed, placed, placed),
        check_vma=False,
    )
```

```python
import functools

import jax
import jax.numpy as jnp
from jax import lax
from jax.experimental import pallas as pl
from jax.experimental.pallas import tpu as pltpu
from jax.sharding import PartitionSpec as P

HORIZON = 3
DT_STEP = 0.25
BOND_SCALE = 5.0
LANES = 128
ROWS = 64
FRAME = 16
OWN = 4
CORE = slice(OWN, OWN + 8)
RIM = 24
DEEP = 32
SHIFTS = (-2, -1, 1, 2)
REACH = range(-HORIZON, HORIZON + 1)


def bond_table():
    table = {}
    number = 0
    for dx in REACH:
        for dy in REACH:
            for dz in REACH:
                radius = dx * dx + dy * dy + dz * dz
                if 0 < radius <= HORIZON * HORIZON and (dx, dy, dz) > (0, 0, 0):
                    table[dx, dy, dz] = (number // 12, number % 12)
                    table[-dx, -dy, -dz] = (6 + number // 12, number % 12)
                    number += 1
    return table


BONDS = bond_table()


def lane_ids():
    return lax.broadcasted_iota(jnp.int32, (8, LANES), 1)


def nothing():
    return jnp.zeros((8, LANES), jnp.float32)


def layer_rows(x):
    return slice(8 * x, 8 * x + 8)


def across(y):
    return pl.ds(y, 8, stride=8)


def rolled(block, shift):
    shift = shift % LANES
    return pltpu.roll(block, shift, axis=1) if shift else block


def z_window(main, side, dz, wide):
    if not wide:
        return rolled(main, -dz)
    lane = lane_ids()
    if dz > 0:
        return rolled(jnp.where(lane < dz, side, main), -dz)
    return rolled(jnp.where(lane >= LANES + dz, side, main), -dz)


def pack_margins(packed, rows, field, group):
    lane = lane_ids()
    start = 4 * (3 * field + group)
    return jnp.where((lane >= start) & (lane < start + 4), rolled(rows, 2 + start), packed)


def unpack_margins(packed, field, group):
    lane = lane_ids()
    return jnp.where((lane >= 126) | (lane < 2), rolled(packed, -(2 + 4 * (3 * field + group))), 0.0)


def bond_sum(offsets, own, words, far, total):
    bases = {}

    def base(axis, step):
        if (axis, step) not in bases:
            bases[axis, step] = own[axis] - float(step) if step else own[axis]
        return bases[axis, step]

    for offset in offsets:
        radius = float(sum(step * step for step in offset))
        word, bit = BONDS[offset]
        there = far(offset)
        stretch = [there[axis] - base(axis, offset[axis]) for axis in range(3)]
        inverse = lax.rsqrt(stretch[0] * stretch[0] + stretch[1] * stretch[1] + stretch[2] * stretch[2])
        factor = (BOND_SCALE / radius - (BOND_SCALE / radius**0.5) * inverse) * there[3]
        factor = jnp.where((words(word) & (1 << bit)) == 0, factor, 0.0)
        total = tuple(total[axis] + factor * stretch[axis] for axis in range(3))
    return total


def advance_kernel(cells_z, disp, vel, mod, field_out, vel_out, msg_out, hold, hold_mod, sem):
    copies = [
        pltpu.make_async_copy(disp, hold, sem.at[0]),
        pltpu.make_async_copy(vel, vel_out, sem.at[1]),
        pltpu.make_async_copy(mod, hold_mod, sem.at[2]),
    ]
    for copy in copies:
        copy.start()
    for copy in copies:
        copy.wait()
    lane = lane_ids()
    for field in range(4):
        packed = nothing()
        for x in range(8):
            rows = layer_rows(x)
            if field < 3:
                own = hold[field, rows] + DT_STEP * vel_out[field, rows]
            else:
                own = jnp.sqrt(hold_mod[rows])
            field_out[field, rows] = own
            top = rolled(own, 8 * x - (cells_z - 3))
            low = rolled(own, 64 + 8 * x)
            packed = jnp.where((lane >= 8 * x) & (lane < 8 * x + 3), top, packed)
            packed = jnp.where((lane >= 64 + 8 * x) & (lane < 64 + 8 * x + 3), low, packed)
        msg_out[field] = packed


def side_kernel(cells_z, fields, arrived, main_out, side_out, low_out, top_out):
    wide = cells_z == LANES
    lane = lane_ids()
    first = cells_z % LANES
    packed = [nothing(), nothing()]
    for field in range(4):
        got = arrived[field]
        for x in range(8):
            rows = layer_rows(x)
            own = fields[field, rows]
            below = rolled(got, 125 - 8 * x)
            above = rolled(got, first - (64 + 8 * x))
            side = jnp.where((lane >= first) & (lane < first + 3), above, 0.0)
            side = jnp.where(lane >= 125, below, side)
            if not wide:
                own = jnp.where(lane < cells_z, own, side)
            main_out[field, rows] = own
            side_out[field, rows] = side
        for face, out in enumerate((low_out, top_out)):
            for r in range(3):
                y = 5 * face + r
                out[RIM * field + 8 * r : RIM * field + 8 * r + 8] = main_out[field, across(y)]
                if wide:
                    packed[face] = pack_margins(packed[face], side_out[field, across(y)], field, r)
    low_out[4 * RIM :] = packed[0]
    top_out[4 * RIM :] = packed[1]


def inside_kernel(wide, main, side, bits, fields, partial_out, next_out, near, far, sem):
    copy = pltpu.make_async_copy(fields.at[:3], next_out, sem)
    copy.start()
    blank = jnp.zeros((OWN, LANES), jnp.float32)
    for field in range(4):
        for x in range(8):
            block = main[field, layer_rows(x)]
            margin = side[field, layer_rows(x)] if wide else None
            for slot, dz in enumerate(SHIFTS):
                near[slot, field, x, :OWN] = blank
                near[slot, field, x, OWN + 8 :] = blank
                near[slot, field, x, CORE] = z_window(block, margin, dz, wide)
            for slot, dz in enumerate((-3, 3)):
                far[slot, field, x] = z_window(block, margin, dz, wide)
    for x in range(8):

        def there(offset, x=x):
            dx, dy, dz = offset
            rows = slice(OWN + dy, OWN + dy + 8)
            if abs(dz) == 3:
                return [far[int(dz > 0), field, x + dx] for field in range(4)]
            return [near[SHIFTS.index(dz), field, x + dx, rows] for field in range(4)]

        rows = layer_rows(x)
        own = [main[field, rows] for field in range(3)]
        offsets = [offset for offset in BONDS if 0 <= x + offset[0] < 8 and offset[2]]
        total = bond_sum(offsets, own, lambda word, rows=rows: bits[word, rows], there, (nothing(),) * 3)
        for axis in range(3):
            partial_out[axis, rows] = total[axis]
    copy.wait()


def deep_kernel(wide, main, side, below, above, low_out, top_out, hold):
    packed = [nothing(), nothing()]
    sources = ((below, 1, 0), (below, 2, 0), (above, 0, 1), (above, 1, 1))
    for field in range(4):
        if wide:
            for face, block in enumerate((below, above)):
                for r in range(3):
                    hold[face, 8 * r : 8 * r + 8] = unpack_margins(block[4 * RIM :], field, r)
        for face, (out, layers) in enumerate(((low_out, (0, 1, 2)), (top_out, (7, 6, 5)))):
            start = DEEP * field
            for depth, x in enumerate(layers):
                out[start + 8 * depth : start + 8 * depth + 8] = main[field, layer_rows(x)]
                if depth == 2:
                    continue
                for place, (block, r, source) in enumerate(sources):
                    row = 4 * depth + place
                    rim = RIM * field + 8 * r + x
                    out[start + 24 + row : start + 25 + row] = block[rim : rim + 1]
                    if wide:
                        hold[2 + face, row : row + 1] = hold[source, 8 * r + x : 8 * r + x + 1]
            if wide:
                for group, x in enumerate(layers[:2]):
                    packed[face] = pack_margins(packed[face], side[field, layer_rows(x)], field, group)
                packed[face] = pack_margins(packed[face], hold[2 + face, :8], field, 2)
    low_out[4 * DEEP :] = packed[0]
    top_out[4 * DEEP :] = packed[1]


def rim_kernel(wide, main, below, above, bits, partial, partial_out, level, frame, near):
    blank = jnp.zeros((OWN, LANES), jnp.float32)
    for field in range(4):
        for x in range(8):
            level[field, x, :OWN] = blank
            level[field, x, CORE] = main[field, layer_rows(x)]
            level[field, x, OWN + 8 :] = blank
    for x in range(8):

        def beside(offset, x=x):
            rows = slice(OWN + offset[1], OWN + offset[1] + 8)
            return [level[field, x + offset[0], rows] for field in range(4)]

        rows = layer_rows(x)
        own = [main[field, rows] for field in range(3)]
        offsets = [offset for offset in BONDS if 0 <= x + offset[0] < 8 and not offset[2]]
        total = tuple(partial[axis, rows] for axis in range(3))
        total = bond_sum(offsets, own, lambda word, rows=rows: bits[word, rows], beside, total)
        for axis in range(3):
            partial_out[axis, rows] = total[axis]
    for face, block in enumerate((below, above)):
        for field in range(4):
            for r in range(3):
                rows = block[RIM * field + 8 * r : RIM * field + 8 * r + 8]
                height = r + 1 if face else 3 - r
                frame[face, height - 1, field, :OWN] = blank
                frame[face, height - 1, field, CORE] = rows
                frame[face, height - 1, field, OWN + 8 :] = blank
                if height == 3:
                    continue
                margin = unpack_margins(block[4 * RIM :], field, r) if wide else None
                for slot, dz in enumerate(SHIFTS):
                    near[slot, face, height - 1, field, :OWN] = blank
                    near[slot, face, height - 1, field, CORE] = z_window(rows, margin, dz, wide)
                    near[slot, face, height - 1, field, OWN + 8 :] = blank
    for face in range(2):
        for depth in range(3):
            y = 7 - depth if face else depth

            def there(offset, face=face, depth=depth):
                dx, dy, dz = offset
                height = abs(dy) - depth - 1
                rows = slice(OWN + dx, OWN + dx + 8)
                if dz == 0:
                    return [frame[face, height, field, rows] for field in range(4)]
                return [near[SHIFTS.index(dz), face, height, field, rows] for field in range(4)]

            own = [main[field, across(y)] for field in range(3)]
            offsets = [offset for offset in BONDS if not 0 <= y + offset[1] < 8]
            total = tuple(partial_out[axis, across(y)] for axis in range(3))
            total = bond_sum(offsets, own, lambda word, y=y: bits[word, across(y)], there, total)
            for axis in range(3):
                partial_out[axis, across(y)] = total[axis]


def face_layers(face):
    return (7, 6, 5) if face else (0, 1, 2)


def face_windows(wide, block, frame, near):
    for field in range(4):
        start = DEEP * field
        groups = [block[start + 8 * group : start + 8 * group + 8] for group in (0, 1, 3)]
        margins = [unpack_margins(block[4 * DEEP :], field, group) if wide else None for group in range(3)]
        views = [(frame, groups)]
        for slot, dz in enumerate(SHIFTS):
            views.append((near.at[slot], [z_window(*pair, dz, wide) for pair in zip(groups, margins)]))
        for ref, parts in views:
            for depth in range(2):
                ref[depth, field, CORE] = parts[depth]
                ref[depth, field, 2:OWN] = parts[2][4 * depth : 4 * depth + 2]
                ref[depth, field, OWN + 8 : 14] = parts[2][4 * depth + 2 : 4 * depth + 4]


def face_sum(face, x, main, block, bits, frame, near, total):
    def there(offset):
        dx, dy, dz = offset
        depth = x + dx - 8 if face else -(x + dx) - 1
        rows = slice(OWN + dy, OWN + dy + 8)
        if depth == 2:
            return [block[DEEP * field + 16 : DEEP * field + 24] for field in range(4)]
        if dz == 0:
            return [frame[depth, field, rows] for field in range(4)]
        return [near[SHIFTS.index(dz), depth, field, rows] for field in range(4)]

    rows = layer_rows(x)
    own = [main[field, rows] for field in range(3)]
    offsets = [offset for offset in BONDS if not 0 <= x + offset[0] < 8 and (offset[0] > 0) == bool(face)]
    return bond_sum(offsets, own, lambda word: bits[word, rows], there, total)


def face_turn(turn):
    place = lax.axis_index("gx")
    odd = place % 2 == 1
    if turn == 0:
        return joined("gx", 0), jnp.logical_not(odd)
    if turn == 1:
        return jnp.logical_and(joined("gx", 1), place >= 2), odd
    early = place < 2
    used = jnp.logical_or(joined("gx", 2), jnp.logical_and(early, joined("gx", 1)))
    return used, jnp.logical_or(early, jnp.logical_not(odd))


def face_kernel(wide, turn, main, block, bits, partial, partial_out, frame, near):
    for axis in range(3):
        for x in range(8):
            partial_out[axis, layer_rows(x)] = partial[axis, layer_rows(x)]
    used, upper = face_turn(turn)
    for face in range(2):

        @pl.when(jnp.logical_and(used, upper if face else jnp.logical_not(upper)))
        def _(face=face):
            face_windows(wide, block, frame, near)
            for x in face_layers(face):
                rows = layer_rows(x)
                total = tuple(partial[axis, rows] for axis in range(3))
                total = face_sum(face, x, main, block, bits, frame, near, total)
                for axis in range(3):
                    partial_out[axis, rows] = total[axis]


def last_face_kernel(
    wide, main, block, bits, vel, partial, force_out, vel_out, frame, near, force_buf, vel_buf, sem
):
    def finish(x, total, copies):
        rows = layer_rows(x)
        root = main[3, rows]
        for axis in range(3):
            force = root * total[axis]
            force_buf[axis, rows] = force
            vel_buf[axis, rows] = vel[axis, rows] + DT_STEP * force
        for slot, (buf, out) in enumerate(((force_buf, force_out), (vel_buf, vel_out))):
            copies.append(pltpu.make_async_copy(buf.at[:, rows], out.at[:, rows], sem.at[slot, x]))
            copies[-1].start()

    used, upper = face_turn(2)

    @pl.when(jnp.logical_not(used))
    def _():
        copies = []
        for x in range(8):
            finish(x, [partial[axis, layer_rows(x)] for axis in range(3)], copies)
        for copy in copies:
            copy.wait()

    for face in range(2):

        @pl.when(jnp.logical_and(used, upper if face else jnp.logical_not(upper)))
        def _(face=face):
            copies = []
            layers = face_layers(face)
            for x in range(8):
                if x not in layers:
                    finish(x, [partial[axis, layer_rows(x)] for axis in range(3)], copies)
            face_windows(wide, block, frame, near)
            for x in layers[::-1]:
                total = tuple(partial[axis, layer_rows(x)] for axis in range(3))
                finish(x, face_sum(face, x, main, block, bits, frame, near, total), copies)
            for copy in copies:
                copy.wait()


VMEM = pl.BlockSpec(memory_space=pltpu.VMEM)
HBM = pl.BlockSpec(memory_space=pltpu.HBM)


def call(kernel, ins, outs, scratch, flops, *operands):
    shapes = [jax.ShapeDtypeStruct(shape, jnp.float32) for shape, _ in outs]
    moved = sum(4 * int(a.size) for a in operands) + sum(4 * int(a.size) for a in shapes)
    return pl.pallas_call(
        kernel,
        out_shape=shapes,
        in_specs=ins,
        out_specs=[place for _, place in outs],
        scratch_shapes=[pltpu.VMEM(a, jnp.float32) if isinstance(a, tuple) else a for a in scratch],
        compiler_params=pltpu.CompilerParams(vmem_limit_bytes=24 * 1024 * 1024),
        cost_estimate=pl.CostEstimate(flops=flops, bytes_accessed=moved, transcendentals=0),
    )(*operands)


AXES = ("gx", "gy", "gz")


def joined(axis, turn):
    place = lax.axis_index(axis)
    start, end = span(lax.axis_size(axis), turn)
    return jnp.logical_and(place >= start, place < end)


def span(count, turn):
    start = turn
    return start, 2 if turn == 0 else start + (count - start) // 2 * 2


def pairs_of(axis, turn):
    sizes = [lax.axis_size(name) for name in AXES]
    which = AXES.index(axis)
    start, end = span(sizes[which], turn)
    stride = 1
    for size in sizes[which + 1 :]:
        stride *= size
    pairs = []
    for device in range(sizes[0] * sizes[1] * sizes[2]):
        place = device // stride % sizes[which]
        if start <= place < end:
            pairs.append((device, device - stride if (place - start) % 2 else device + stride))
        elif axis != "gz" and sizes[2] % 2 == 0:
            pairs.append((device, device ^ 1))
    return pairs


def traded(low, top, axis):
    even = lax.axis_index(axis) % 2 == 0
    outer, inner = jnp.where(even, top, low), jnp.where(even, low, top)
    return [lax.ppermute(block, AXES, pairs_of(axis, turn)) for turn, block in enumerate((outer, inner, outer))]


def sorted_out(axis, got):
    place = lax.axis_index(axis)
    outer = jnp.where(place < 2, got[0], got[2])
    outer = jnp.where(jnp.logical_or(joined(axis, 0), joined(axis, 2)), outer, 0.0)
    inner = jnp.where(joined(axis, 1), got[1], 0.0)
    even = place % 2 == 0
    return jnp.where(even, inner, outer), jnp.where(even, outer, inner)


def body(displacement, velocity, micromodulus, damage_bits):
    cells_z = micromodulus.shape[2]
    wide = cells_z == LANES
    if not wide:
        pad = [(0, 0), (0, 0), (0, 0), (0, LANES - cells_z)]
        displacement, velocity, damage_bits = (
            jnp.pad(a, pad) for a in (displacement, velocity, damage_bits)
        )
        micromodulus = jnp.pad(micromodulus, pad[1:])
    shape = displacement.shape
    displacement = displacement.reshape(3, ROWS, LANES)
    velocity = velocity.reshape(3, ROWS, LANES)
    micromodulus = micromodulus.reshape(ROWS, LANES)
    damage_bits = damage_bits.reshape(12, ROWS, LANES)
    vectors = (3, ROWS, LANES)
    all_fields = (4, ROWS, LANES)
    fields, kept, z_msg = call(
        functools.partial(advance_kernel, cells_z),
        [HBM] * 3,
        [(all_fields, VMEM), (vectors, VMEM), ((4, 8, LANES), VMEM)],
        [vectors, (ROWS, LANES), pltpu.SemaphoreType.DMA((3,))],
        100_000,
        *(pltpu.with_memory_space_constraint(a, pltpu.HBM) for a in (displacement, velocity, micromodulus)),
    )
    first_half = lax.broadcasted_iota(jnp.int32, z_msg.shape, 2) < 64
    place = lax.axis_index("gz")
    if lax.axis_size("gz") == 2:
        other = lax.ppermute(z_msg, "gz", [(0, 1), (1, 0)])
        z_got = jnp.where(first_half == (place == 1), other, 0.0)
    else:
        before, after = sorted_out("gz", traded(z_msg, z_msg, "gz"))
        z_got = jnp.where(first_half, before, after)
    rim_msg = ((4 * RIM + 8, LANES), VMEM)
    main, side, low, top = call(
        functools.partial(side_kernel, cells_z),
        [VMEM] * 2,
        [(all_fields, VMEM), (all_fields, VMEM), rim_msg, rim_msg],
        [],
        100_000,
        fields,
        z_got,
    )
    got = traded(low, top, "gy")
    partial, advanced = call(
        functools.partial(inside_kernel, wide),
        [VMEM] * 4,
        [(vectors, VMEM), (vectors, HBM)],
        [(4, 4, 8, FRAME, LANES), (2, 4, 8, 8, LANES), pltpu.SemaphoreType.DMA],
        20_000_000,
        main,
        side,
        damage_bits,
        fields,
    )
    first, second, third, partial = lax.optimization_barrier((got[0], got[1], got[2], partial))
    below, above = sorted_out("gy", (first, second, third))
    deep_msg = ((4 * DEEP + 8, LANES), VMEM)
    low, top = call(
        functools.partial(deep_kernel, wide),
        [VMEM] * 4,
        [deep_msg, deep_msg],
        [(4, RIM, LANES)],
        100_000,
        main,
        side,
        below,
        above,
    )
    got = traded(low, top, "gx")
    (partial,) = call(
        functools.partial(rim_kernel, wide),
        [VMEM] * 5,
        [(vectors, VMEM)],
        [(4, 8, FRAME, LANES), (2, 3, 4, FRAME, LANES), (4, 2, 2, 4, FRAME, LANES)],
        4_000_000,
        main,
        below,
        above,
        damage_bits,
        partial,
    )
    windows = [(2, 4, FRAME, LANES), (4, 2, 4, FRAME, LANES)]
    for turn in range(2):
        (partial,) = call(
            functools.partial(face_kernel, wide, turn),
            [VMEM] * 4,
            [(vectors, VMEM)],
            windows,
            2_000_000,
            main,
            got[turn],
            damage_bits,
            partial,
        )
    last = jnp.where(lax.axis_index("gx") < 2, got[1], got[2])
    force, moved = call(
        functools.partial(last_face_kernel, wide),
        [VMEM] * 5,
        [(vectors, HBM), (vectors, HBM)],
        [*windows, vectors, vectors, pltpu.SemaphoreType.DMA((2, 8))],
        2_000_000,
        main,
        last,
        damage_bits,
        kept,
        partial,
    )
    return tuple(a.reshape(shape)[..., :cells_z] for a in (force, advanced, moved))


def solution(mesh):
    placed = P(None, "gx", "gy", "gz")
    return jax.shard_map(
        body,
        mesh=mesh,
        in_specs=(placed, placed, P("gx", "gy", "gz"), placed),
        out_specs=(placed, placed, placed),
        check_vma=False,
    )
```

```python
import functools

import jax
import jax.numpy as jnp
from jax import lax
from jax.experimental import pallas as pl
from jax.experimental.pallas import tpu as pltpu
from jax.sharding import PartitionSpec as P

HORIZON = 3
DT_STEP = 0.25
BOND_SCALE = 5.0
LANES = 128
ROWS = 64
FRAME = 16
OWN = 4
CORE = slice(OWN, OWN + 8)
RIM = 24
DEEP = 32
SHIFTS = (-2, -1, 1, 2)
REACH = range(-HORIZON, HORIZON + 1)


def bond_table():
    table = {}
    number = 0
    for dx in REACH:
        for dy in REACH:
            for dz in REACH:
                radius = dx * dx + dy * dy + dz * dz
                if 0 < radius <= HORIZON * HORIZON and (dx, dy, dz) > (0, 0, 0):
                    table[dx, dy, dz] = (number // 12, number % 12)
                    table[-dx, -dy, -dz] = (6 + number // 12, number % 12)
                    number += 1
    return table


BONDS = bond_table()


def lane_ids():
    return lax.broadcasted_iota(jnp.int32, (8, LANES), 1)


def nothing():
    return jnp.zeros((8, LANES), jnp.float32)


def layer_rows(x):
    return slice(8 * x, 8 * x + 8)


def across(y):
    return pl.ds(y, 8, stride=8)


def rolled(block, shift):
    shift = shift % LANES
    return pltpu.roll(block, shift, axis=1) if shift else block


def z_window(main, side, dz, wide):
    if not wide:
        return rolled(main, -dz)
    lane = lane_ids()
    if dz > 0:
        return rolled(jnp.where(lane < dz, side, main), -dz)
    return rolled(jnp.where(lane >= LANES + dz, side, main), -dz)


def pack_margins(packed, rows, field, group):
    lane = lane_ids()
    start = 4 * (3 * field + group)
    return jnp.where((lane >= start) & (lane < start + 4), rolled(rows, 2 + start), packed)


def unpack_margins(packed, field, group):
    lane = lane_ids()
    return jnp.where((lane >= 126) | (lane < 2), rolled(packed, -(2 + 4 * (3 * field + group))), 0.0)


def bond_sum(offsets, own, words, far, total):
    bases = {}

    def base(axis, step):
        if (axis, step) not in bases:
            bases[axis, step] = own[axis] - float(step) if step else own[axis]
        return bases[axis, step]

    for offset in offsets:
        radius = float(sum(step * step for step in offset))
        word, bit = BONDS[offset]
        there = far(offset)
        stretch = [there[axis] - base(axis, offset[axis]) for axis in range(3)]
        inverse = lax.rsqrt(stretch[0] * stretch[0] + stretch[1] * stretch[1] + stretch[2] * stretch[2])
        factor = (BOND_SCALE / radius - (BOND_SCALE / radius**0.5) * inverse) * there[3]
        factor = jnp.where((words(word) & (1 << bit)) == 0, factor, 0.0)
        total = tuple(total[axis] + factor * stretch[axis] for axis in range(3))
    return total


def rim_lane(field, x):
    return 4 * (8 * field + x)


def advance_kernel(cells_z, paired, disp, vel, mod, field_out, vel_out, *rest):
    msg_out, (hold, hold_mod, sem) = rest[:-3], rest[-3:]
    copies = [
        pltpu.make_async_copy(disp, hold, sem.at[0]),
        pltpu.make_async_copy(vel, vel_out, sem.at[1]),
        pltpu.make_async_copy(mod, hold_mod, sem.at[2]),
    ]
    for copy in copies:
        copy.start()
    for copy in copies:
        copy.wait()
    if paired:
        starts = [jnp.where(lax.axis_index("gz") == 0, cells_z - 3, 0)]
    else:
        starts = [0, cells_z - 3]
    lane = lane_ids()
    packed = [nothing() for _ in starts]
    for field in (3, 0, 1, 2):
        for x in range(8):
            rows = layer_rows(x)
            if field < 3:
                own = hold[field, rows] + DT_STEP * vel_out[field, rows]
            else:
                own = jnp.sqrt(hold_mod[rows])
            field_out[field, rows] = own
            place = rim_lane(field, x)
            for side, start in enumerate(starts):
                moved = pltpu.roll(own, (place - start + LANES) % LANES, axis=1)
                packed[side] = jnp.where((lane >= place) & (lane < place + 3), moved, packed[side])
    for out, block in zip(msg_out, packed):
        out[...] = block


def side_kernel(cells_z, paired, fields, *rest):
    arrived, (main_out, side_out, low_out, top_out) = rest[:-4], rest[-4:]
    wide = cells_z == LANES
    lane = lane_ids()
    first = cells_z % LANES
    starts = [jnp.where(lax.axis_index("gz") == 0, first, 125)] if paired else [125, first]
    masks = [(lane >= start) & (lane < start + 3) for start in starts]
    blocks = [ref[...] for ref in arrived]
    packed = [nothing(), nothing()]
    for field in range(4):
        for x in range(8):
            rows = layer_rows(x)
            own = fields[field, rows]
            side = nothing()
            for block, start, mask in zip(blocks, starts, masks):
                moved = pltpu.roll(block, (start - rim_lane(field, x) + LANES) % LANES, axis=1)
                side = jnp.where(mask, moved, side)
            if not wide:
                own = jnp.where(lane < cells_z, own, side)
            main_out[field, rows] = own
            side_out[field, rows] = side
        for face, out in enumerate((low_out, top_out)):
            for r in range(3):
                y = 5 * face + r
                out[RIM * field + 8 * r : RIM * field + 8 * r + 8] = main_out[field, across(y)]
                if wide:
                    packed[face] = pack_margins(packed[face], side_out[field, across(y)], field, r)
    low_out[4 * RIM :] = packed[0]
    top_out[4 * RIM :] = packed[1]


def inside_kernel(wide, main, side, bits, fields, partial_out, next_out, near, far, sem):
    copy = pltpu.make_async_copy(fields.at[:3], next_out, sem)
    copy.start()
    blank = jnp.zeros((OWN, LANES), jnp.float32)
    for field in range(4):
        for x in range(8):
            block = main[field, layer_rows(x)]
            margin = side[field, layer_rows(x)] if wide else None
            for slot, dz in enumerate(SHIFTS):
                near[slot, field, x, :OWN] = blank
                near[slot, field, x, OWN + 8 :] = blank
                near[slot, field, x, CORE] = z_window(block, margin, dz, wide)
            for slot, dz in enumerate((-3, 3)):
                far[slot, field, x] = z_window(block, margin, dz, wide)
    for x in range(8):

        def there(offset, x=x):
            dx, dy, dz = offset
            rows = slice(OWN + dy, OWN + dy + 8)
            if abs(dz) == 3:
                return [far[int(dz > 0), field, x + dx] for field in range(4)]
            return [near[SHIFTS.index(dz), field, x + dx, rows] for field in range(4)]

        rows = layer_rows(x)
        own = [main[field, rows] for field in range(3)]
        offsets = [offset for offset in BONDS if 0 <= x + offset[0] < 8 and offset[2]]
        total = bond_sum(offsets, own, lambda word, rows=rows: bits[word, rows], there, (nothing(),) * 3)
        for axis in range(3):
            partial_out[axis, rows] = total[axis]
    copy.wait()


def deep_kernel(wide, main, side, below, above, low_out, top_out, hold):
    packed = [nothing(), nothing()]
    sources = ((below, 1, 0), (below, 2, 0), (above, 0, 1), (above, 1, 1))
    for field in range(4):
        if wide:
            for face, block in enumerate((below, above)):
                for r in range(3):
                    hold[face, 8 * r : 8 * r + 8] = unpack_margins(block[4 * RIM :], field, r)
        for face, (out, layers) in enumerate(((low_out, (0, 1, 2)), (top_out, (7, 6, 5)))):
            start = DEEP * field
            for depth, x in enumerate(layers):
                out[start + 8 * depth : start + 8 * depth + 8] = main[field, layer_rows(x)]
                if depth == 2:
                    continue
                for place, (block, r, source) in enumerate(sources):
                    row = 4 * depth + place
                    rim = RIM * field + 8 * r + x
                    out[start + 24 + row : start + 25 + row] = block[rim : rim + 1]
                    if wide:
                        hold[2 + face, row : row + 1] = hold[source, 8 * r + x : 8 * r + x + 1]
            if wide:
                for group, x in enumerate(layers[:2]):
                    packed[face] = pack_margins(packed[face], side[field, layer_rows(x)], field, group)
                packed[face] = pack_margins(packed[face], hold[2 + face, :8], field, 2)
    low_out[4 * DEEP :] = packed[0]
    top_out[4 * DEEP :] = packed[1]


def rim_kernel(wide, main, below, above, bits, partial, partial_out, level, frame, near):
    blank = jnp.zeros((OWN, LANES), jnp.float32)
    for field in range(4):
        for x in range(8):
            level[field, x, :OWN] = blank
            level[field, x, CORE] = main[field, layer_rows(x)]
            level[field, x, OWN + 8 :] = blank
    for x in range(8):

        def beside(offset, x=x):
            rows = slice(OWN + offset[1], OWN + offset[1] + 8)
            return [level[field, x + offset[0], rows] for field in range(4)]

        rows = layer_rows(x)
        own = [main[field, rows] for field in range(3)]
        offsets = [offset for offset in BONDS if 0 <= x + offset[0] < 8 and not offset[2]]
        total = tuple(partial[axis, rows] for axis in range(3))
        total = bond_sum(offsets, own, lambda word, rows=rows: bits[word, rows], beside, total)
        for axis in range(3):
            partial_out[axis, rows] = total[axis]
    for face, block in enumerate((below, above)):
        for field in range(4):
            for r in range(3):
                rows = block[RIM * field + 8 * r : RIM * field + 8 * r + 8]
                height = r + 1 if face else 3 - r
                frame[face, height - 1, field, :OWN] = blank
                frame[face, height - 1, field, CORE] = rows
                frame[face, height - 1, field, OWN + 8 :] = blank
                if height == 3:
                    continue
                margin = unpack_margins(block[4 * RIM :], field, r) if wide else None
                for slot, dz in enumerate(SHIFTS):
                    near[slot, face, height - 1, field, :OWN] = blank
                    near[slot, face, height - 1, field, CORE] = z_window(rows, margin, dz, wide)
                    near[slot, face, height - 1, field, OWN + 8 :] = blank
    for face in range(2):
        for depth in range(3):
            y = 7 - depth if face else depth

            def there(offset, face=face, depth=depth):
                dx, dy, dz = offset
                height = abs(dy) - depth - 1
                rows = slice(OWN + dx, OWN + dx + 8)
                if dz == 0:
                    return [frame[face, height, field, rows] for field in range(4)]
                return [near[SHIFTS.index(dz), face, height, field, rows] for field in range(4)]

            own = [main[field, across(y)] for field in range(3)]
            offsets = [offset for offset in BONDS if not 0 <= y + offset[1] < 8]
            total = tuple(partial_out[axis, across(y)] for axis in range(3))
            total = bond_sum(offsets, own, lambda word, y=y: bits[word, across(y)], there, total)
            for axis in range(3):
                partial_out[axis, across(y)] = total[axis]


def face_layers(face):
    return (7, 6, 5) if face else (0, 1, 2)


def face_windows(wide, block, frame, near):
    for field in range(4):
        start = DEEP * field
        groups = [block[start + 8 * group : start + 8 * group + 8] for group in (0, 1, 3)]
        margins = [unpack_margins(block[4 * DEEP :], field, group) if wide else None for group in range(3)]
        views = [(frame, groups)]
        for slot, dz in enumerate(SHIFTS):
            views.append((near.at[slot], [z_window(*pair, dz, wide) for pair in zip(groups, margins)]))
        for ref, parts in views:
            for depth in range(2):
                ref[depth, field, CORE] = parts[depth]
                ref[depth, field, 2:OWN] = parts[2][4 * depth : 4 * depth + 2]
                ref[depth, field, OWN + 8 : 14] = parts[2][4 * depth + 2 : 4 * depth + 4]


def face_sum(face, x, main, block, bits, frame, near, total):
    def there(offset):
        dx, dy, dz = offset
        depth = x + dx - 8 if face else -(x + dx) - 1
        rows = slice(OWN + dy, OWN + dy + 8)
        if depth == 2:
            return [block[DEEP * field + 16 : DEEP * field + 24] for field in range(4)]
        if dz == 0:
            return [frame[depth, field, rows] for field in range(4)]
        return [near[SHIFTS.index(dz), depth, field, rows] for field in range(4)]

    rows = layer_rows(x)
    own = [main[field, rows] for field in range(3)]
    offsets = [offset for offset in BONDS if not 0 <= x + offset[0] < 8 and (offset[0] > 0) == bool(face)]
    return bond_sum(offsets, own, lambda word: bits[word, rows], there, total)


def face_turn(turn):
    place = lax.axis_index("gx")
    odd = place % 2 == 1
    if turn == 0:
        return joined("gx", 0), jnp.logical_not(odd)
    if turn == 1:
        return jnp.logical_and(joined("gx", 1), place >= 2), odd
    early = place < 2
    used = jnp.logical_or(joined("gx", 2), jnp.logical_and(early, joined("gx", 1)))
    return used, jnp.logical_or(early, jnp.logical_not(odd))


def face_kernel(wide, turn, main, block, bits, partial, partial_out, frame, near):
    for axis in range(3):
        for x in range(8):
            partial_out[axis, layer_rows(x)] = partial[axis, layer_rows(x)]
    used, upper = face_turn(turn)
    for face in range(2):

        @pl.when(jnp.logical_and(used, upper if face else jnp.logical_not(upper)))
        def _(face=face):
            face_windows(wide, block, frame, near)
            for x in face_layers(face):
                rows = layer_rows(x)
                total = tuple(partial[axis, rows] for axis in range(3))
                total = face_sum(face, x, main, block, bits, frame, near, total)
                for axis in range(3):
                    partial_out[axis, rows] = total[axis]


def last_face_kernel(
    wide, main, block, bits, vel, partial, force_out, vel_out, frame, near, force_buf, vel_buf, sem
):
    def finish(x, total, copies):
        rows = layer_rows(x)
        root = main[3, rows]
        for axis in range(3):
            force = root * total[axis]
            force_buf[axis, rows] = force
            vel_buf[axis, rows] = vel[axis, rows] + DT_STEP * force
        for slot, (buf, out) in enumerate(((force_buf, force_out), (vel_buf, vel_out))):
            copies.append(pltpu.make_async_copy(buf.at[:, rows], out.at[:, rows], sem.at[slot, x]))
            copies[-1].start()

    used, upper = face_turn(2)

    @pl.when(jnp.logical_not(used))
    def _():
        copies = []
        for x in range(8):
            finish(x, [partial[axis, layer_rows(x)] for axis in range(3)], copies)
        for copy in copies:
            copy.wait()

    for face in range(2):

        @pl.when(jnp.logical_and(used, upper if face else jnp.logical_not(upper)))
        def _(face=face):
            copies = []
            layers = face_layers(face)
            for x in range(8):
                if x not in layers:
                    finish(x, [partial[axis, layer_rows(x)] for axis in range(3)], copies)
            face_windows(wide, block, frame, near)
            for x in layers[::-1]:
                total = tuple(partial[axis, layer_rows(x)] for axis in range(3))
                finish(x, face_sum(face, x, main, block, bits, frame, near, total), copies)
            for copy in copies:
                copy.wait()


VMEM = pl.BlockSpec(memory_space=pltpu.VMEM)
HBM = pl.BlockSpec(memory_space=pltpu.HBM)


def call(kernel, ins, outs, scratch, flops, *operands):
    shapes = [jax.ShapeDtypeStruct(shape, jnp.float32) for shape, _ in outs]
    moved = sum(4 * int(a.size) for a in operands) + sum(4 * int(a.size) for a in shapes)
    return pl.pallas_call(
        kernel,
        out_shape=shapes,
        in_specs=ins,
        out_specs=[place for _, place in outs],
        scratch_shapes=[pltpu.VMEM(a, jnp.float32) if isinstance(a, tuple) else a for a in scratch],
        compiler_params=pltpu.CompilerParams(vmem_limit_bytes=24 * 1024 * 1024),
        cost_estimate=pl.CostEstimate(flops=flops, bytes_accessed=moved, transcendentals=0),
    )(*operands)


AXES = ("gx", "gy", "gz")


def joined(axis, turn):
    place = lax.axis_index(axis)
    start, end = span(lax.axis_size(axis), turn)
    return jnp.logical_and(place >= start, place < end)


def span(count, turn):
    start = turn
    return start, min(2, count // 2 * 2) if turn == 0 else start + (count - start) // 2 * 2


def pairs_of(axis, turn):
    sizes = [lax.axis_size(name) for name in AXES]
    which = AXES.index(axis)
    start, end = span(sizes[which], turn)
    stride = 1
    for size in sizes[which + 1 :]:
        stride *= size
    pairs = []
    for device in range(sizes[0] * sizes[1] * sizes[2]):
        place = device // stride % sizes[which]
        if start <= place < end:
            pairs.append((device, device - stride if (place - start) % 2 else device + stride))
        elif axis != "gz" and sizes[2] % 2 == 0:
            pairs.append((device, device ^ 1))
    return pairs


def traded(low, top, axis):
    even = lax.axis_index(axis) % 2 == 0
    outer, inner = jnp.where(even, top, low), jnp.where(even, low, top)
    return [lax.ppermute(block, AXES, pairs_of(axis, turn)) for turn, block in enumerate((outer, inner, outer))]


def sorted_out(axis, got):
    place = lax.axis_index(axis)
    outer = jnp.where(place < 2, got[0], got[2])
    outer = jnp.where(jnp.logical_or(joined(axis, 0), joined(axis, 2)), outer, 0.0)
    inner = jnp.where(joined(axis, 1), got[1], 0.0)
    even = place % 2 == 0
    return jnp.where(even, inner, outer), jnp.where(even, outer, inner)


def body(displacement, velocity, micromodulus, damage_bits):
    cells_z = micromodulus.shape[2]
    wide = cells_z == LANES
    if not wide:
        pad = [(0, 0), (0, 0), (0, 0), (0, LANES - cells_z)]
        displacement, velocity, damage_bits = (
            jnp.pad(a, pad) for a in (displacement, velocity, damage_bits)
        )
        micromodulus = jnp.pad(micromodulus, pad[1:])
    shape = displacement.shape
    displacement = displacement.reshape(3, ROWS, LANES)
    velocity = velocity.reshape(3, ROWS, LANES)
    micromodulus = micromodulus.reshape(ROWS, LANES)
    damage_bits = damage_bits.reshape(12, ROWS, LANES)
    vectors = (3, ROWS, LANES)
    all_fields = (4, ROWS, LANES)
    paired = lax.axis_size("gz") == 2
    z_msg = ((8, LANES), VMEM)
    fields, kept, *z_sent = call(
        functools.partial(advance_kernel, cells_z, paired),
        [HBM] * 3,
        [(all_fields, VMEM), (vectors, VMEM), *[z_msg] * (1 if paired else 2)],
        [vectors, (ROWS, LANES), pltpu.SemaphoreType.DMA((3,))],
        100_000,
        *(pltpu.with_memory_space_constraint(a, pltpu.HBM) for a in (displacement, velocity, micromodulus)),
    )
    if paired:
        z_got = [lax.ppermute(z_sent[0], "gz", [(0, 1), (1, 0)])]
    else:
        z_got = sorted_out("gz", traded(*z_sent, "gz"))
    rim_msg = ((4 * RIM + 8, LANES), VMEM)
    main, side, low, top = call(
        functools.partial(side_kernel, cells_z, paired),
        [VMEM] * (1 + len(z_got)),
        [(all_fields, VMEM), (all_fields, VMEM), rim_msg, rim_msg],
        [],
        100_000,
        fields,
        *z_got,
    )
    got = traded(low, top, "gy")
    partial, advanced = call(
        functools.partial(inside_kernel, wide),
        [VMEM] * 4,
        [(vectors, VMEM), (vectors, HBM)],
        [(4, 4, 8, FRAME, LANES), (2, 4, 8, 8, LANES), pltpu.SemaphoreType.DMA],
        20_000_000,
        main,
        side,
        damage_bits,
        fields,
    )
    first, second, third, partial = lax.optimization_barrier((got[0], got[1], got[2], partial))
    below, above = sorted_out("gy", (first, second, third))
    deep_msg = ((4 * DEEP + 8, LANES), VMEM)
    low, top = call(
        functools.partial(deep_kernel, wide),
        [VMEM] * 4,
        [deep_msg, deep_msg],
        [(4, RIM, LANES)],
        100_000,
        main,
        side,
        below,
        above,
    )
    got = traded(low, top, "gx")
    (partial,) = call(
        functools.partial(rim_kernel, wide),
        [VMEM] * 5,
        [(vectors, VMEM)],
        [(4, 8, FRAME, LANES), (2, 3, 4, FRAME, LANES), (4, 2, 2, 4, FRAME, LANES)],
        4_000_000,
        main,
        below,
        above,
        damage_bits,
        partial,
    )
    windows = [(2, 4, FRAME, LANES), (4, 2, 4, FRAME, LANES)]
    for turn in range(2):
        (partial,) = call(
            functools.partial(face_kernel, wide, turn),
            [VMEM] * 4,
            [(vectors, VMEM)],
            windows,
            2_000_000,
            main,
            got[turn],
            damage_bits,
            partial,
        )
    last = jnp.where(lax.axis_index("gx") < 2, got[1], got[2])
    force, moved = call(
        functools.partial(last_face_kernel, wide),
        [VMEM] * 5,
        [(vectors, HBM), (vectors, HBM)],
        [*windows, vectors, vectors, pltpu.SemaphoreType.DMA((2, 8))],
        2_000_000,
        main,
        last,
        damage_bits,
        kept,
        partial,
    )
    return tuple(a.reshape(shape)[..., :cells_z] for a in (force, advanced, moved))


def solution(mesh):
    placed = P(None, "gx", "gy", "gz")
    return jax.shard_map(
        body,
        mesh=mesh,
        in_specs=(placed, placed, P("gx", "gy", "gz"), placed),
        out_specs=(placed, placed, placed),
        check_vma=False,
    )
```

```python
import functools

import jax
import jax.numpy as jnp
from jax import lax
from jax.experimental import pallas as pl
from jax.experimental.pallas import tpu as pltpu
from jax.sharding import PartitionSpec as P

HORIZON = 3
DT_STEP = 0.25
BOND_SCALE = 5.0
LANES = 128
ROWS = 64
FRAME = 16
OWN = 4
CORE = slice(OWN, OWN + 8)
RIM = 24
DEEP = 32
SHIFTS = (-2, -1, 1, 2)
REACH = range(-HORIZON, HORIZON + 1)


def bond_table():
    table = {}
    number = 0
    for dx in REACH:
        for dy in REACH:
            for dz in REACH:
                radius = dx * dx + dy * dy + dz * dz
                if 0 < radius <= HORIZON * HORIZON and (dx, dy, dz) > (0, 0, 0):
                    table[dx, dy, dz] = (number // 12, number % 12)
                    table[-dx, -dy, -dz] = (6 + number // 12, number % 12)
                    number += 1
    return table


BONDS = bond_table()


def lane_ids():
    return lax.broadcasted_iota(jnp.int32, (8, LANES), 1)


def nothing():
    return jnp.zeros((8, LANES), jnp.float32)


def layer_rows(x):
    return slice(8 * x, 8 * x + 8)


def across(y):
    return pl.ds(y, 8, stride=8)


def rolled(block, shift):
    shift = shift % LANES
    return pltpu.roll(block, shift, axis=1) if shift else block


def z_window(main, side, dz, wide):
    if not wide:
        return rolled(main, -dz)
    lane = lane_ids()
    if dz > 0:
        return rolled(jnp.where(lane < dz, side, main), -dz)
    return rolled(jnp.where(lane >= LANES + dz, side, main), -dz)


def pack_margins(packed, rows, field, group):
    lane = lane_ids()
    start = 4 * (3 * field + group)
    return jnp.where((lane >= start) & (lane < start + 4), rolled(rows, 2 + start), packed)


def unpack_margins(packed, field, group):
    lane = lane_ids()
    return jnp.where((lane >= 126) | (lane < 2), rolled(packed, -(2 + 4 * (3 * field + group))), 0.0)


def bond_sum(offsets, own, words, far, total):
    bases = {}

    def base(axis, step):
        if (axis, step) not in bases:
            bases[axis, step] = own[axis] - float(step) if step else own[axis]
        return bases[axis, step]

    for offset in offsets:
        radius = float(sum(step * step for step in offset))
        word, bit = BONDS[offset]
        there = far(offset)
        stretch = [there[axis] - base(axis, offset[axis]) for axis in range(3)]
        inverse = lax.rsqrt(stretch[0] * stretch[0] + stretch[1] * stretch[1] + stretch[2] * stretch[2])
        factor = (BOND_SCALE / radius - (BOND_SCALE / radius**0.5) * inverse) * there[3]
        factor = jnp.where((words(word) & (1 << bit)) == 0, factor, 0.0)
        total = tuple(total[axis] + factor * stretch[axis] for axis in range(3))
    return total


def rim_lane(field, x):
    return 4 * (8 * field + x)


def advance_kernel(cells_z, paired, disp, vel, mod, field_out, vel_out, *rest):
    msg_out, (hold, hold_mod, sem) = rest[:-3], rest[-3:]
    copies = [
        pltpu.make_async_copy(mod, hold_mod, sem.at[0]),
        pltpu.make_async_copy(disp, hold, sem.at[1]),
        pltpu.make_async_copy(vel, vel_out, sem.at[2]),
    ]
    for copy in copies:
        copy.start()
    if paired:
        starts = [jnp.where(lax.axis_index("gz") == 0, cells_z - 3, 0)]
    else:
        starts = [0, cells_z - 3]
    lane = lane_ids()
    packed = [nothing() for _ in starts]
    for field in (3, 0, 1, 2):
        for copy in {3: copies[:1], 0: copies[1:]}.get(field, ()):
            copy.wait()
        for x in range(8):
            rows = layer_rows(x)
            if field < 3:
                own = hold[field, rows] + DT_STEP * vel_out[field, rows]
            else:
                own = jnp.sqrt(hold_mod[rows])
            field_out[field, rows] = own
            place = rim_lane(field, x)
            for side, start in enumerate(starts):
                moved = pltpu.roll(own, (place - start + LANES) % LANES, axis=1)
                packed[side] = jnp.where((lane >= place) & (lane < place + 3), moved, packed[side])
    for out, block in zip(msg_out, packed):
        out[...] = block


def side_kernel(cells_z, paired, fields, *rest):
    arrived, (main_out, side_out, low_out, top_out) = rest[:-4], rest[-4:]
    wide = cells_z == LANES
    lane = lane_ids()
    first = cells_z % LANES
    starts = [jnp.where(lax.axis_index("gz") == 0, first, 125)] if paired else [125, first]
    masks = [(lane >= start) & (lane < start + 3) for start in starts]
    blocks = [ref[...] for ref in arrived]
    packed = [nothing(), nothing()]
    for field in range(4):
        for x in range(8):
            rows = layer_rows(x)
            own = fields[field, rows]
            side = nothing()
            for block, start, mask in zip(blocks, starts, masks):
                moved = pltpu.roll(block, (start - rim_lane(field, x) + LANES) % LANES, axis=1)
                side = jnp.where(mask, moved, side)
            if not wide:
                own = jnp.where(lane < cells_z, own, side)
            main_out[field, rows] = own
            side_out[field, rows] = side
        for face, out in enumerate((low_out, top_out)):
            for r in range(3):
                y = 5 * face + r
                out[RIM * field + 8 * r : RIM * field + 8 * r + 8] = main_out[field, across(y)]
                if wide:
                    packed[face] = pack_margins(packed[face], side_out[field, across(y)], field, r)
    low_out[4 * RIM :] = packed[0]
    top_out[4 * RIM :] = packed[1]


def inside_kernel(wide, main, side, bits, fields, partial_out, next_out, near, far, sem):
    copy = pltpu.make_async_copy(fields.at[:3], next_out, sem)
    copy.start()
    blank = jnp.zeros((OWN, LANES), jnp.float32)
    for field in range(4):
        for x in range(8):
            block = main[field, layer_rows(x)]
            margin = side[field, layer_rows(x)] if wide else None
            for slot, dz in enumerate(SHIFTS):
                near[slot, field, x, :OWN] = blank
                near[slot, field, x, OWN + 8 :] = blank
                near[slot, field, x, CORE] = z_window(block, margin, dz, wide)
            for slot, dz in enumerate((-3, 3)):
                far[slot, field, x] = z_window(block, margin, dz, wide)
    for x in range(8):

        def there(offset, x=x):
            dx, dy, dz = offset
            rows = slice(OWN + dy, OWN + dy + 8)
            if abs(dz) == 3:
                return [far[int(dz > 0), field, x + dx] for field in range(4)]
            return [near[SHIFTS.index(dz), field, x + dx, rows] for field in range(4)]

        rows = layer_rows(x)
        own = [main[field, rows] for field in range(3)]
        offsets = [offset for offset in BONDS if 0 <= x + offset[0] < 8 and offset[2]]
        total = bond_sum(offsets, own, lambda word, rows=rows: bits[word, rows], there, (nothing(),) * 3)
        for axis in range(3):
            partial_out[axis, rows] = total[axis]
    copy.wait()


def deep_kernel(wide, main, side, below, above, low_out, top_out, hold):
    packed = [nothing(), nothing()]
    sources = ((below, 1, 0), (below, 2, 0), (above, 0, 1), (above, 1, 1))
    for field in range(4):
        if wide:
            for face, block in enumerate((below, above)):
                for r in range(3):
                    hold[face, 8 * r : 8 * r + 8] = unpack_margins(block[4 * RIM :], field, r)
        for face, (out, layers) in enumerate(((low_out, (0, 1, 2)), (top_out, (7, 6, 5)))):
            start = DEEP * field
            for depth, x in enumerate(layers):
                out[start + 8 * depth : start + 8 * depth + 8] = main[field, layer_rows(x)]
                if depth == 2:
                    continue
                for place, (block, r, source) in enumerate(sources):
                    row = 4 * depth + place
                    rim = RIM * field + 8 * r + x
                    out[start + 24 + row : start + 25 + row] = block[rim : rim + 1]
                    if wide:
                        hold[2 + face, row : row + 1] = hold[source, 8 * r + x : 8 * r + x + 1]
            if wide:
                for group, x in enumerate(layers[:2]):
                    packed[face] = pack_margins(packed[face], side[field, layer_rows(x)], field, group)
                packed[face] = pack_margins(packed[face], hold[2 + face, :8], field, 2)
    low_out[4 * DEEP :] = packed[0]
    top_out[4 * DEEP :] = packed[1]


def rim_kernel(wide, main, below, above, bits, partial, partial_out, level, frame, near):
    blank = jnp.zeros((OWN, LANES), jnp.float32)
    for field in range(4):
        for x in range(8):
            level[field, x, :OWN] = blank
            level[field, x, CORE] = main[field, layer_rows(x)]
            level[field, x, OWN + 8 :] = blank
    for x in range(8):

        def beside(offset, x=x):
            rows = slice(OWN + offset[1], OWN + offset[1] + 8)
            return [level[field, x + offset[0], rows] for field in range(4)]

        rows = layer_rows(x)
        own = [main[field, rows] for field in range(3)]
        offsets = [offset for offset in BONDS if 0 <= x + offset[0] < 8 and not offset[2]]
        total = tuple(partial[axis, rows] for axis in range(3))
        total = bond_sum(offsets, own, lambda word, rows=rows: bits[word, rows], beside, total)
        for axis in range(3):
            partial_out[axis, rows] = total[axis]
    for face, block in enumerate((below, above)):
        for field in range(4):
            for r in range(3):
                rows = block[RIM * field + 8 * r : RIM * field + 8 * r + 8]
                height = r + 1 if face else 3 - r
                frame[face, height - 1, field, :OWN] = blank
                frame[face, height - 1, field, CORE] = rows
                frame[face, height - 1, field, OWN + 8 :] = blank
                if height == 3:
                    continue
                margin = unpack_margins(block[4 * RIM :], field, r) if wide else None
                for slot, dz in enumerate(SHIFTS):
                    near[slot, face, height - 1, field, :OWN] = blank
                    near[slot, face, height - 1, field, CORE] = z_window(rows, margin, dz, wide)
                    near[slot, face, height - 1, field, OWN + 8 :] = blank
    for face in range(2):
        for depth in range(3):
            y = 7 - depth if face else depth

            def there(offset, face=face, depth=depth):
                dx, dy, dz = offset
                height = abs(dy) - depth - 1
                rows = slice(OWN + dx, OWN + dx + 8)
                if dz == 0:
                    return [frame[face, height, field, rows] for field in range(4)]
                return [near[SHIFTS.index(dz), face, height, field, rows] for field in range(4)]

            own = [main[field, across(y)] for field in range(3)]
            offsets = [offset for offset in BONDS if not 0 <= y + offset[1] < 8]
            total = tuple(partial_out[axis, across(y)] for axis in range(3))
            total = bond_sum(offsets, own, lambda word, y=y: bits[word, across(y)], there, total)
            for axis in range(3):
                partial_out[axis, across(y)] = total[axis]


def face_layers(face):
    return (7, 6, 5) if face else (0, 1, 2)


def face_windows(wide, block, frame, near):
    for field in range(4):
        start = DEEP * field
        groups = [block[start + 8 * group : start + 8 * group + 8] for group in (0, 1, 3)]
        margins = [unpack_margins(block[4 * DEEP :], field, group) if wide else None for group in range(3)]
        views = [(frame, groups)]
        for slot, dz in enumerate(SHIFTS):
            views.append((near.at[slot], [z_window(*pair, dz, wide) for pair in zip(groups, margins)]))
        for ref, parts in views:
            for depth in range(2):
                ref[depth, field, CORE] = parts[depth]
                ref[depth, field, 2:OWN] = parts[2][4 * depth : 4 * depth + 2]
                ref[depth, field, OWN + 8 : 14] = parts[2][4 * depth + 2 : 4 * depth + 4]


def face_sum(face, x, main, block, bits, frame, near, total):
    def there(offset):
        dx, dy, dz = offset
        depth = x + dx - 8 if face else -(x + dx) - 1
        rows = slice(OWN + dy, OWN + dy + 8)
        if depth == 2:
            return [block[DEEP * field + 16 : DEEP * field + 24] for field in range(4)]
        if dz == 0:
            return [frame[depth, field, rows] for field in range(4)]
        return [near[SHIFTS.index(dz), depth, field, rows] for field in range(4)]

    rows = layer_rows(x)
    own = [main[field, rows] for field in range(3)]
    offsets = [offset for offset in BONDS if not 0 <= x + offset[0] < 8 and (offset[0] > 0) == bool(face)]
    return bond_sum(offsets, own, lambda word: bits[word, rows], there, total)


def face_turn(turn):
    place = lax.axis_index("gx")
    odd = place % 2 == 1
    if turn == 0:
        return joined("gx", 0), jnp.logical_not(odd)
    if turn == 1:
        return jnp.logical_and(joined("gx", 1), place >= 2), odd
    early = place < 2
    used = jnp.logical_or(joined("gx", 2), jnp.logical_and(early, joined("gx", 1)))
    return used, jnp.logical_or(early, jnp.logical_not(odd))


def face_kernel(wide, turn, main, block, bits, partial, partial_out, frame, near):
    for axis in range(3):
        for x in range(8):
            partial_out[axis, layer_rows(x)] = partial[axis, layer_rows(x)]
    used, upper = face_turn(turn)
    for face in range(2):

        @pl.when(jnp.logical_and(used, upper if face else jnp.logical_not(upper)))
        def _(face=face):
            face_windows(wide, block, frame, near)
            for x in face_layers(face):
                rows = layer_rows(x)
                total = tuple(partial[axis, rows] for axis in range(3))
                total = face_sum(face, x, main, block, bits, frame, near, total)
                for axis in range(3):
                    partial_out[axis, rows] = total[axis]


def last_face_kernel(
    wide, main, block, bits, vel, partial, force_out, vel_out, frame, near, force_buf, vel_buf, sem
):
    def finish(x, total):
        rows = layer_rows(x)
        root = main[3, rows]
        for axis in range(3):
            force = root * total[axis]
            force_buf[axis, rows] = force
            vel_buf[axis, rows] = vel[axis, rows] + DT_STEP * force

    def send(first, last, copies):
        rows = slice(8 * first, 8 * last)
        for slot, (buf, out) in enumerate(((force_buf, force_out), (vel_buf, vel_out))):
            copies.append(pltpu.make_async_copy(buf.at[:, rows], out.at[:, rows], sem.at[slot, first]))
            copies[-1].start()

    used, upper = face_turn(2)

    @pl.when(jnp.logical_not(used))
    def _():
        copies = []
        for x in range(8):
            finish(x, [partial[axis, layer_rows(x)] for axis in range(3)])
        send(0, 8, copies)
        for copy in copies:
            copy.wait()

    for face in range(2):

        @pl.when(jnp.logical_and(used, upper if face else jnp.logical_not(upper)))
        def _(face=face):
            copies = []
            layers = face_layers(face)
            face_windows(wide, block, frame, near)
            for x in range(8):
                if x not in layers:
                    finish(x, [partial[axis, layer_rows(x)] for axis in range(3)])
            send(*((0, 5) if face else (3, 8)), copies)
            for x in layers[::-1]:
                total = tuple(partial[axis, layer_rows(x)] for axis in range(3))
                finish(x, face_sum(face, x, main, block, bits, frame, near, total))
                send(x, x + 1, copies)
            for copy in copies:
                copy.wait()


VMEM = pl.BlockSpec(memory_space=pltpu.VMEM)
HBM = pl.BlockSpec(memory_space=pltpu.HBM)


def call(kernel, ins, outs, scratch, flops, *operands):
    shapes = [jax.ShapeDtypeStruct(shape, jnp.float32) for shape, _ in outs]
    moved = sum(4 * int(a.size) for a in operands) + sum(4 * int(a.size) for a in shapes)
    return pl.pallas_call(
        kernel,
        out_shape=shapes,
        in_specs=ins,
        out_specs=[place for _, place in outs],
        scratch_shapes=[pltpu.VMEM(a, jnp.float32) if isinstance(a, tuple) else a for a in scratch],
        compiler_params=pltpu.CompilerParams(vmem_limit_bytes=24 * 1024 * 1024),
        cost_estimate=pl.CostEstimate(flops=flops, bytes_accessed=moved, transcendentals=0),
    )(*operands)


AXES = ("gx", "gy", "gz")


def joined(axis, turn):
    place = lax.axis_index(axis)
    start, end = span(lax.axis_size(axis), turn)
    return jnp.logical_and(place >= start, place < end)


def span(count, turn):
    start = turn
    return start, min(2, count // 2 * 2) if turn == 0 else start + (count - start) // 2 * 2


def pairs_of(axis, turn):
    sizes = [lax.axis_size(name) for name in AXES]
    which = AXES.index(axis)
    start, end = span(sizes[which], turn)
    stride = 1
    for size in sizes[which + 1 :]:
        stride *= size
    pairs = []
    for device in range(sizes[0] * sizes[1] * sizes[2]):
        place = device // stride % sizes[which]
        if start <= place < end:
            pairs.append((device, device - stride if (place - start) % 2 else device + stride))
        elif axis != "gz" and sizes[2] % 2 == 0:
            pairs.append((device, device ^ 1))
    return pairs


def traded(low, top, axis):
    even = lax.axis_index(axis) % 2 == 0
    outer, inner = jnp.where(even, top, low), jnp.where(even, low, top)
    return [lax.ppermute(block, AXES, pairs_of(axis, turn)) for turn, block in enumerate((outer, inner, outer))]


def sorted_out(axis, got):
    place = lax.axis_index(axis)
    outer = jnp.where(place < 2, got[0], got[2])
    outer = jnp.where(jnp.logical_or(joined(axis, 0), joined(axis, 2)), outer, 0.0)
    inner = jnp.where(joined(axis, 1), got[1], 0.0)
    even = place % 2 == 0
    return jnp.where(even, inner, outer), jnp.where(even, outer, inner)


def body(displacement, velocity, micromodulus, damage_bits):
    cells_z = micromodulus.shape[2]
    wide = cells_z == LANES
    if not wide:
        pad = [(0, 0), (0, 0), (0, 0), (0, LANES - cells_z)]
        displacement, velocity, damage_bits = (
            jnp.pad(a, pad) for a in (displacement, velocity, damage_bits)
        )
        micromodulus = jnp.pad(micromodulus, pad[1:])
    shape = displacement.shape
    displacement = displacement.reshape(3, ROWS, LANES)
    velocity = velocity.reshape(3, ROWS, LANES)
    micromodulus = micromodulus.reshape(ROWS, LANES)
    damage_bits = damage_bits.reshape(12, ROWS, LANES)
    vectors = (3, ROWS, LANES)
    all_fields = (4, ROWS, LANES)
    paired = lax.axis_size("gz") == 2
    z_msg = ((8, LANES), VMEM)
    fields, kept, *z_sent = call(
        functools.partial(advance_kernel, cells_z, paired),
        [HBM] * 3,
        [(all_fields, VMEM), (vectors, VMEM), *[z_msg] * (1 if paired else 2)],
        [vectors, (ROWS, LANES), pltpu.SemaphoreType.DMA((3,))],
        100_000,
        *(pltpu.with_memory_space_constraint(a, pltpu.HBM) for a in (displacement, velocity, micromodulus)),
    )
    if paired:
        z_got = [lax.ppermute(z_sent[0], "gz", [(0, 1), (1, 0)])]
    else:
        z_got = sorted_out("gz", traded(*z_sent, "gz"))
    rim_msg = ((4 * RIM + 8, LANES), VMEM)
    main, side, low, top = call(
        functools.partial(side_kernel, cells_z, paired),
        [VMEM] * (1 + len(z_got)),
        [(all_fields, VMEM), (all_fields, VMEM), rim_msg, rim_msg],
        [],
        100_000,
        fields,
        *z_got,
    )
    got = traded(low, top, "gy")
    partial, advanced = call(
        functools.partial(inside_kernel, wide),
        [VMEM] * 4,
        [(vectors, VMEM), (vectors, HBM)],
        [(4, 4, 8, FRAME, LANES), (2, 4, 8, 8, LANES), pltpu.SemaphoreType.DMA],
        20_000_000,
        main,
        side,
        damage_bits,
        fields,
    )
    first, second, third, partial = lax.optimization_barrier((got[0], got[1], got[2], partial))
    below, above = sorted_out("gy", (first, second, third))
    deep_msg = ((4 * DEEP + 8, LANES), VMEM)
    low, top = call(
        functools.partial(deep_kernel, wide),
        [VMEM] * 4,
        [deep_msg, deep_msg],
        [(4, RIM, LANES)],
        100_000,
        main,
        side,
        below,
        above,
    )
    got = traded(low, top, "gx")
    (partial,) = call(
        functools.partial(rim_kernel, wide),
        [VMEM] * 5,
        [(vectors, VMEM)],
        [(4, 8, FRAME, LANES), (2, 3, 4, FRAME, LANES), (4, 2, 2, 4, FRAME, LANES)],
        4_000_000,
        main,
        below,
        above,
        damage_bits,
        partial,
    )
    windows = [(2, 4, FRAME, LANES), (4, 2, 4, FRAME, LANES)]
    for turn in range(2):
        (partial,) = call(
            functools.partial(face_kernel, wide, turn),
            [VMEM] * 4,
            [(vectors, VMEM)],
            windows,
            2_000_000,
            main,
            got[turn],
            damage_bits,
            partial,
        )
    last = jnp.where(lax.axis_index("gx") < 2, got[1], got[2])
    force, moved = call(
        functools.partial(last_face_kernel, wide),
        [VMEM] * 5,
        [(vectors, HBM), (vectors, HBM)],
        [*windows, vectors, vectors, pltpu.SemaphoreType.DMA((2, 8))],
        2_000_000,
        main,
        last,
        damage_bits,
        kept,
        partial,
    )
    return tuple(a.reshape(shape)[..., :cells_z] for a in (force, advanced, moved))


def solution(mesh):
    placed = P(None, "gx", "gy", "gz")
    return jax.shard_map(
        body,
        mesh=mesh,
        in_specs=(placed, placed, P("gx", "gy", "gz"), placed),
        out_specs=(placed, placed, placed),
        check_vma=False,
    )
```
